256 devices in a mesh: seq: 32 (over z_hi, x, core), head: 8 (over z_lo, y).
Axes of the slice: x: 4, y: 4, z: 8 (z_hi: 4, z_lo: 2; z = z_hi * 2 + z_lo), core: 2. Of those that a mesh axis runs over, the one named last changes fastest.
Arguments:
- query_src: bfloat16 [8192, 5120], P(('seq', 'head')), may hold values from -18 to 18
- key_src: bfloat16 [8192, 5120], P(('seq', 'head')), may hold values from -9 to 9
- value_src: bfloat16 [8192, 5120], P(('seq', 'head')), may hold values from -6 to 6
- value_edit: bfloat16 [8192, 5120], P(('seq', 'head')), may hold values from -6 to 6
- tile_mask: int32 [128, 128], P('seq'), may hold values from 0 to 1, as said below
- word_map: int32 [8192], P(('seq', 'head')), may hold values from 0 to 511
- blend_table: float32 [512, 40], replicated, may hold values from 0.1 to 0.9
Outputs:
- edited: bfloat16 [8192, 5120], P(('seq', 'head'))
The draws below stay inside these ranges and needn't reach their ends.
Inputs may be any that keep to these rules, and one draw needn't show every extreme that they name: `tile_mask`: every diagonal entry is 1.
All inputs are finite; a program needn't handle non-finite values.
Results may differ from the reference program's by a relative error of at most 0.012.
Values may be sent and summed in bfloat16 or wider, within the bound.
A program may use at most 128 MiB of HBM per device.

```python
import math
import jax
import jax.numpy as jnp
import numpy as np
from jax import lax

HEADS = 40
HEAD_DIM = 128
WORDS = 512
TILE = 64
BLK = 256
D = 5120
TOKENS = 8192


def draw_query_src(key, part):
    key = jax.random.fold_in(key, 11)
    values = jnp.clip(1.5 * jax.random.normal(key, (TOKENS, D), jnp.float32), -9.0, 9.0)
    return values.astype(jnp.bfloat16)


def draw_key_src(key, part):
    key = jax.random.fold_in(key, 12)
    values = jnp.clip(1.5 * jax.random.normal(key, (TOKENS, D), jnp.float32), -9.0, 9.0)
    return values.astype(jnp.bfloat16)


def draw_tile_mask(key, part):
    key = jax.random.fold_in(key, 5)
    tile_count = TOKENS // TILE
    block_of = jnp.arange(tile_count, dtype=jnp.int32) * TILE // BLK
    block_total = TOKENS // BLK
    levels = 1 + 7 * block_of // max(block_total - 1, 1)
    random_ints = jax.random.randint(key, (tile_count, tile_count), 0, 8)
    diagonal = jnp.arange(tile_count)[:, None] == jnp.arange(tile_count)[None, :]
    return jnp.logical_or(random_ints < levels[:, None], diagonal).astype(jnp.int32)


def touch_ends(values, rng, least, largest):
    longest = values.shape.index(max(values.shape))
    spots = []
    for shift in (0, 1):
        where = [jax.random.randint(jax.random.fold_in(rng, axis), (), 0, length) for axis, length in enumerate(values.shape)]
        where[longest] = (where[longest] + shift) % values.shape[longest]
        spots.append(tuple(where))
    return values.at[spots[0]].set(least).at[spots[1]].set(largest)


def block_scale(stream_key, shape, split, low, top_value):
    def one(dim, shards_of):
        draws = jax.random.uniform(jax.random.fold_in(jax.random.fold_in(stream_key, 6), dim), (shards_of,), jnp.float32, low / len(split), top_value / len(split))
        return jnp.repeat(jnp.exp(draws), shape[dim] // shards_of).reshape((-1,) + (1,) * (len(shape) - dim - 1))

    factor_of = one(*split[0])
    for cut in split[1:]:
        factor_of = factor_of * one(*cut)
    return factor_of


def cumulative_ranks(amount, slope):
    portions = [(1 << 20) // math.isqrt(standing ** slope) + 1 for standing in range(1, amount + 1)]
    spread = 1 + sum(portions) // (1 << 30)
    return np.cumsum(np.array([max(1, weight // spread) for weight in portions]))


def ranked_ids(key, dims, count, lean):
    listing = cumulative_ranks(count, lean)
    lot = jax.random.randint(jax.random.fold_in(key, 1), dims, 0, int(listing[count - 1]))
    rank = jnp.searchsorted(jnp.asarray(listing, jnp.int32), lot, side="right")
    return jax.random.permutation(jax.random.fold_in(key, 2), count)[rank].astype(jnp.int32)


def bell_draw(rng, shape, deviation, most, shards=(), held_as=jnp.bfloat16):
    values = deviation * jax.random.normal(rng, shape, jnp.float32)
    if shards:
        values = values * block_scale(rng, shape, shards, -0.22, 0.18)
    return jnp.clip(values, -most, most).astype(held_as)


def setup_inputs(seed: int = 0) -> dict:
    keys = jax.random.split(jax.random.key(seed), 8)
    query_src = draw_query_src(jax.random.fold_in(keys[7], 71), 0)
    key_src = draw_key_src(jax.random.fold_in(keys[7], 71), 0)
    value_src = bell_draw(keys[2], (TOKENS, D), 1.0, 6.0, ((0, 256),))
    value_edit = bell_draw(keys[3], (TOKENS, D), 1.0, 6.0, ((0, 256),))
    tile_mask = draw_tile_mask(jax.random.fold_in(keys[7], 71), 0)
    word_map = touch_ends(ranked_ids(keys[5], (TOKENS,), WORDS, 2), jax.random.fold_in(keys[5], 3), 0, WORDS - 1).astype(jnp.int32)
    blend_table = jnp.clip(jax.random.uniform(keys[6], (WORDS, HEADS), jnp.float32, 0.1, 0.9), 0.1, 0.9)
    return {"query_src": query_src, "key_src": key_src, "value_src": value_src, "value_edit": value_edit, "tile_mask": tile_mask, "word_map": word_map, "blend_table": blend_table}


def reference(query_src, key_src, value_src, value_edit, tile_mask, word_map, blend_table):
    token_count = query_src.shape[0]

    def heads_first(array):
        return array.reshape(token_count, HEADS, HEAD_DIM).transpose(1, 0, 2)

    queries = heads_first(query_src)
    key_rows = heads_first(key_src)
    value_rows = jnp.concatenate([heads_first(value_src), heads_first(value_edit)], axis=2)
    allowed = jnp.repeat(jnp.repeat(tile_mask > 0, TILE, axis=0), TILE, axis=1)
    score_scale = HEAD_DIM ** -0.5

    def one_head(operands):
        head_q, head_k, head_v = operands
        scores = jnp.dot(head_q, head_k.T, preferred_element_type=jnp.float32) * score_scale
        masked = jnp.where(allowed, scores, -1e30)
        row_max = jnp.max(masked, axis=1, keepdims=True)
        weights = jnp.where(allowed, jnp.exp(masked - row_max), 0.0)
        totals = jnp.sum(weights, axis=1, keepdims=True)
        numerators = jnp.dot(weights.astype(jnp.bfloat16), head_v, preferred_element_type=jnp.float32)
        return numerators / totals

    results = lax.map(one_head, (queries, key_rows, value_rows)).transpose(1, 0, 2)
    mixing = blend_table[word_map][:, :, None]
    mixed = mixing * results[:, :, HEAD_DIM:] + (1.0 - mixing) * results[:, :, :HEAD_DIM]
    return mixed.astype(jnp.bfloat16).reshape(token_count, HEADS * HEAD_DIM)
```

```python
import jax
import jax.numpy as jnp
from jax import lax
from jax.experimental import pallas as pl
from jax.experimental.pallas import tpu as pltpu
from jax.sharding import PartitionSpec as P

MESH = pl.DeviceIdType.MESH
HD = 128
NX, NY, NZ, NC = 4, 4, 8, 2
HZ = 5
TB = 32
SLOTS = 11
ROWS = SLOTS * 4 * TB
CK = 1024
QC = 352
MASKED = -(2.0**100)
OFFS = (0, 1, -1, 2, -2, 3, -3, 4)
LOG2E = 1.4426950408889634


def offset_of(s):
    half = (s + 1) // 2
    return half * (2 * (s % 2) - 1)


def copy_wait(ref, sem):
    pltpu.make_async_copy(ref, ref, sem).wait()


def body(
    q_ref, k_ref, v_ref, w_ref, ext_ref, out_ref,
    zq, zx, zkv, hq, hx, hk, qb, xb, kv, oh, qa, mix, mm, ll, oo, ro, ox,
    zq_s, zq_r, zx_s, zx_r, zk_s, zk_r,
    pq_s, pq_r, pqe_r, px_s, px_r, pxe_r, bq_s, bq_r, bx_s, bx_r,
    p1_s, p1_r, p1e_r, p2_s, p2e_s, p2_r, c_s, c_r,
    r1_s, r1_r, rb_s, rb_r, re_s, re_r, r2_s, r2_r,
):
    seq = lax.axis_index("seq")
    head = lax.axis_index("head")
    z = (seq // 8) * 2 + head // 4
    x = (seq // 2) % 4
    c = seq % 2
    y = head % 4
    last = y == 3

    def dev(dx, dy, dz, dc):
        return ((dz // 2) * 8 + dx * 2 + dc, (dz % 2) * 4 + dy)

    def send(src, dst, ss, rs, to):
        pltpu.make_async_remote_copy(
            src_ref=src, dst_ref=dst, send_sem=ss, recv_sem=rs, device_id=to, device_id_type=MESH
        ).start()

    def local(src, dst, rs):
        pltpu.make_async_copy(src, dst, rs).start()

    def wait_send(src, ss):
        copy_wait(src, ss)

    def cols(ref3, zz, count):
        return ref3.at[:, pl.ds(pl.multiple_of(zz * (HZ * HD), HD), count * HD)]

    def lanes(j):
        return pl.ds(pl.multiple_of(j * HD, HD), HD)

    def block(i):
        return pl.ds(pl.multiple_of(i * TB, TB), TB)

    barrier = pltpu.get_barrier_semaphore()
    for d in range(1, NZ):
        pl.semaphore_signal(barrier, inc=1, device_id=dev(x, y, (z + d) % NZ, c), device_id_type=MESH)
    for d in range(1, NX * NY):
        pl.semaphore_signal(
            barrier, inc=1, device_id=dev((x + d // 4) % 4, (y + d % 4) % 4, z, c), device_id_type=MESH
        )
    pl.semaphore_signal(barrier, inc=1, device_id=dev(x, y, z, 1 - c), device_id_type=MESH)
    pl.semaphore_wait(barrier, NZ + NX * NY - 1)

    local(cols(q_ref, z, HZ), zq.at[z], zq_r.at[z])
    local(ext_ref.at[z], zx.at[z], zx_r.at[z])
    for s in range(1, NZ):
        to = (z - OFFS[s] + NZ) % NZ
        send(cols(q_ref, to, HZ), zq.at[z], zq_s.at[s], zq_r.at[z], dev(x, y, to, c))
        send(ext_ref.at[to], zx.at[z], zx_s.at[s], zx_r.at[z], dev(x, y, to, c))
    for i, ref in enumerate((k_ref, v_ref, w_ref)):
        local(cols(ref, z, HZ), zkv.at[z, i], zk_r.at[z])
    for s in range(1, NZ):
        to = (z - OFFS[s] + NZ) % NZ
        for i, ref in enumerate((k_ref, v_ref, w_ref)):
            send(cols(ref, to, HZ), zkv.at[z, i], zk_s.at[s], zk_r.at[z], dev(x, y, to, c))

    row = lax.broadcasted_iota(jnp.int32, (CK, HD), 0)
    lane = lax.broadcasted_iota(jnp.int32, (CK, HD), 1)
    from_line, inner = (row // 128) % 4, (row // TB) % 4
    row_x = jnp.where(last, from_line, inner)
    row_y = jnp.where(last, inner, from_line)
    tile = row_x * 8 + (row // 512) * 4 + row_y // 2

    def fill_onehot(zz, carry):
        base = (zz // 2) * 32 + (zz % 2) * 2
        oh[zz] = jnp.where(lane - base == tile, 1.0, 0.0).astype(jnp.bfloat16)
        return carry

    lax.fori_loop(0, NZ, fill_onehot, 0)
    mm[...] = jnp.full(mm.shape, MASKED, jnp.float32)
    ll[...] = jnp.zeros(ll.shape, jnp.float32)

    def clear(i, carry):
        oo[pl.ds(pl.multiple_of(i * 128, 128), 128), :] = jnp.zeros((128, 2 * HD), jnp.float32)
        return carry

    lax.fori_loop(0, SLOTS, clear, 0)

    @pl.when(y >= 2)
    def _():
        qb[10] = jnp.zeros(qb.shape[1:], qb.dtype)
        xb[10] = jnp.zeros(xb.shape[1:], xb.dtype)

    @pl.when(last)
    def _():
        qb[8:10] = jnp.zeros((2,) + qb.shape[1:], qb.dtype)
        xb[8:10] = jnp.zeros((2,) + xb.shape[1:], xb.dtype)

    def spread_queries():
        for i in range(NZ):
            copy_wait(zq.at[i], zq_r.at[i])
            copy_wait(zx.at[i], zx_r.at[i])

        def to_lines(qdst, xdst):
            local(zq.at[:, :, lanes(x)], qdst, pq_r.at[x])
            local(zx, xdst, px_r.at[x])
            for d in range(1, 4):
                j = (x + d) % 4
                send(zq.at[:, :, lanes(j)], qdst, pq_s.at[d], pq_r.at[x], dev(j, y, z, c))
                send(zx, xdst, px_s.at[d], px_r.at[x], dev(j, y, z, c))

        @pl.when(last)
        def _():
            to_lines(hq.at[:, block(x), :], hx.at[:, x])
            local(zq.at[:, :, pl.ds(4 * HD, HD)], qb.at[pl.ds(0, 8), pl.ds(3 * TB, TB), :], pqe_r.at[3])
            local(zx, xb.at[pl.ds(0, 8), 3], pxe_r.at[3])

        @pl.when(jnp.logical_not(last))
        def _():
            to_lines(qb.at[pl.ds(0, 8), block(x), :], xb.at[pl.ds(0, 8), x])
            send(
                zq.at[:, :, pl.ds(4 * HD, HD)], qb.at[pl.ds(0, 8), block(y), :],
                pq_s.at[0], pqe_r.at[y], dev(x, 3, z, c),
            )
            send(zx, xb.at[pl.ds(0, 8), y], px_s.at[0], pxe_r.at[y], dev(x, 3, z, c))

    def lend_queries():
        for i in range(4):
            copy_wait(hq.at[:, pl.ds(0, TB), :], pq_r.at[i])
            copy_wait(zx, px_r.at[i])

        @pl.when(last)
        def _():
            for t in range(3):
                n = 3 if t < 2 else 2
                send(hq.at[pl.ds(3 * t, n)], qb.at[pl.ds(8, n)], bq_s.at[t], bq_r, dev(x, t, z, c))
                send(hx.at[pl.ds(3 * t, n)], xb.at[pl.ds(8, n)], bx_s.at[t], bx_r, dev(x, t, z, c))
            for i in range(4):
                copy_wait(hq.at[:, pl.ds(0, TB), :], pqe_r.at[i])
                copy_wait(zx, pxe_r.at[i])

    def ready_queries():
        @pl.when(y < 2)
        def _():
            copy_wait(qb.at[pl.ds(8, 3)], bq_r)
            copy_wait(xb.at[pl.ds(8, 3)], bx_r)

        @pl.when(y == 2)
        def _():
            copy_wait(qb.at[pl.ds(8, 2)], bq_r)
            copy_wait(xb.at[pl.ds(8, 2)], bx_r)

        which = 1 + jnp.where(last, 4, x)
        sub = lax.broadcasted_iota(jnp.int32, (4, 8, 128), 1)
        diag = lax.broadcasted_iota(jnp.int32, (4, TB, 128), 1) == lax.broadcasted_iota(
            jnp.int32, (4, TB, 128), 2
        )

        def one(i, carry):
            rows = pl.ds(pl.multiple_of(i * 128, 128), 128)
            extra = xb[i]
            qa[rows, 0:HD] = qb[i]
            bias = jnp.broadcast_to(extra[:, 0:1, :], (4, TB, 128))
            qa[rows, HD : 2 * HD] = bias.reshape(128, 128).astype(jnp.bfloat16)
            shares = jnp.sum(jnp.where(sub == which, extra, 0.0), axis=1, keepdims=True)
            column = jnp.sum(jnp.where(diag, shares, 0.0), axis=2, keepdims=True)
            mix[rows, :] = jnp.broadcast_to(column, (4, TB, 128)).reshape(128, 128)
            return carry

        lax.fori_loop(0, SLOTS, one, 0)

    def source(s):
        return (z + offset_of(s) + NZ) % NZ

    def stage_one(s):
        zz = source(s)
        copy_wait(zkv.at[zz], zk_r.at[zz])

        def to_lines(dst):
            local(zkv.at[zz, :, :, lanes(x)], dst, p1_r.at[s, x])
            for d in range(1, 4):
                j = (x + d) % 4
                send(zkv.at[zz, :, :, lanes(j)], dst, p1_s.at[s, d], p1_r.at[s, x], dev(j, y, z, c))

        @pl.when(last)
        def _():
            to_lines(hk.at[zz, :, block(x), :])
            local(
                zkv.at[zz, :, :, pl.ds(4 * HD, HD)], kv.at[zz, :, c, x, pl.ds(3 * TB, TB), :], p1e_r.at[s, 3]
            )

        @pl.when(jnp.logical_not(last))
        def _():
            to_lines(kv.at[zz, :, c, y, block(x), :])
            send(
                zkv.at[zz, :, :, pl.ds(4 * HD, HD)], kv.at[zz, :, c, x, block(y), :],
                p1_s.at[s, 0], p1e_r.at[s, y], dev(x, 3, z, c),
            )

    def stage_two(s):
        zz = source(s)
        piece = hk.at[zz, :, pl.ds(0, TB), :]
        for i in range(4):
            copy_wait(piece, p1_r.at[s, i])

        @pl.when(last)
        def _():
            for t in range(3):
                send(hk.at[zz], kv.at[zz, :, c, 3], p2_s.at[s, t], p2_r.at[s, 3], dev(x, t, z, c))
            for i in range(4):
                copy_wait(piece, p1e_r.at[s, i])
            own = kv.at[zz, :, c, x]
            for d in range(1, 4):
                send(own, own, p2e_s.at[s, d], p2_r.at[s, x], dev((x + d) % 4, y, z, c))

        @pl.when(jnp.logical_not(last))
        def _():
            own = kv.at[zz, :, c, y]
            for d in range(1, 3):
                send(own, own, p2_s.at[s, d], p2_r.at[s, y], dev(x, (y + d) % 3, z, c))

    def stage_three(s):
        zz = source(s)
        own = jnp.where(last, x, y)
        for d in range(1, 4):
            copy_wait(hk.at[zz], p2_r.at[s, (own + d) % 4])
        half = kv.at[zz, :, c]
        send(half, half, c_s.at[s], c_r.at[s], dev(x, y, z, 1 - c))

    scale = HD ** (-0.5) * LOG2E

    def attend(s):
        zz = source(s)
        copy_wait(kv.at[zz, :, 0], c_r.at[s])

        def some_rows(i, carry):
            rows = pl.ds(pl.multiple_of(i * QC, 32), QC)
            keys = jnp.concatenate([kv[zz, 0].reshape(CK, HD), oh[zz]], axis=1)
            values = jnp.concatenate([kv[zz, 1].reshape(CK, HD), kv[zz, 2].reshape(CK, HD)], axis=1)
            scores = lax.dot_general(
                qa[rows, :], keys, (((1,), (1,)), ((), ())), preferred_element_type=jnp.float32
            )
            old = mm[rows, :]
            new = jnp.maximum(old, jnp.max(scores, axis=1, keepdims=True))
            weights = jnp.exp2((scores - new[:, 0:1]) * scale)
            shrink = jnp.exp2((old - new) * scale)
            part = weights[:, 0:128]
            for t in range(1, CK // 128):
                part = part + weights[:, t * 128 : (t + 1) * 128]
            mm[rows, :] = new
            ll[rows, :] = ll[rows, :] * shrink + part
            sums = jnp.dot(weights.astype(jnp.bfloat16), values, preferred_element_type=jnp.float32)
            oo[rows, :] = oo[rows, :] * jnp.concatenate([shrink, shrink], axis=1) + sums
            return carry

        lax.fori_loop(0, ROWS // QC, some_rows, 0)

    spread_queries()
    stage_one(0)
    lend_queries()
    stage_one(1)
    stage_two(0)
    ready_queries()
    stage_one(2)
    stage_two(1)
    stage_three(0)

    def step(t, carry):
        attend(t)

        @pl.when(t + 3 < NZ)
        def _():
            stage_one(t + 3)

        @pl.when(t + 2 < NZ)
        def _():
            stage_two(t + 2)

        @pl.when(t + 1 < NZ)
        def _():
            stage_three(t + 1)

        return carry

    lax.fori_loop(0, NZ, step, 0)

    def finish(i, carry):
        rows = pl.ds(pl.multiple_of(i * 128, 128), 128)
        total = jnp.sum(ll[rows, :], axis=1, keepdims=True)
        share = mix[rows, :]
        both = oo[rows, :] / total
        ro[i] = (share * both[:, HD:] + (1.0 - share) * both[:, :HD]).astype(jnp.bfloat16)
        return carry

    lax.fori_loop(0, SLOTS, finish, 0)

    @pl.when(last)
    def _():
        e_lanes = pl.ds(4 * HD, HD)
        local(ro.at[pl.ds(0, 8), pl.ds(3 * TB, TB), :], ox.at[:, :, e_lanes], re_r)
        for t in range(3):
            send(ro.at[pl.ds(0, 8), pl.ds(t * TB, TB), :], ox.at[:, :, e_lanes], r1_s.at[t], re_r, dev(x, t, z, c))
        for j in range(4):
            for t in range(3):
                n = 3 if t < 2 else 2
                copy_wait(ox.at[pl.ds(3 * t, n), :, lanes(j)], rb_r.at[j, t])

    @pl.when(jnp.logical_not(last))
    def _():
        mine = lanes(x)
        local(ro.at[pl.ds(0, 8), block(x), :], ox.at[:, :, mine], r1_r.at[x])
        for d in range(1, 4):
            j = (x + d) % 4
            send(ro.at[pl.ds(0, 8), block(j), :], ox.at[:, :, mine], r1_s.at[d], r1_r.at[x], dev(j, y, z, c))
        for i in range(4):

            @pl.when(y < 2)
            def _():
                send(
                    ro.at[pl.ds(8, 3), pl.ds(i * TB, TB), :], ox.at[pl.ds(3 * y, 3), :, mine],
                    rb_s.at[i], rb_r.at[x, y], dev(i, 3, z, c),
                )

            @pl.when(y == 2)
            def _():
                send(
                    ro.at[pl.ds(8, 2), pl.ds(i * TB, TB), :], ox.at[pl.ds(6, 2), :, mine],
                    rb_s.at[i], rb_r.at[x, 2], dev(i, 3, z, c),
                )

        for i in range(4):
            copy_wait(ox.at[:, :, lanes(i)], r1_r.at[i])

    copy_wait(ox.at[:, :, pl.ds(4 * HD, HD)], re_r)
    target = cols(out_ref, z, HZ)
    local(ox.at[z], target, r2_r.at[z])
    for s in range(1, NZ):
        to = (z - OFFS[s] + NZ) % NZ
        send(ox.at[to], target, r2_s.at[s], r2_r.at[z], dev(x, y, to, c))

    for s in range(1, NZ):
        wait_send(zq.at[0], zq_s.at[s])
        wait_send(zx.at[0], zx_s.at[s])
        wait_send(zkv.at[0], zk_s.at[s])
    for d in range(1, 4):
        wait_send(hq.at[:, pl.ds(0, TB), :], pq_s.at[d])
        wait_send(zx, px_s.at[d])

    def left(s, carry):
        for d in range(1, 4):
            wait_send(hk.at[0, :, pl.ds(0, TB), :], p1_s.at[s, d])
        wait_send(kv.at[0, :, 0], c_s.at[s])

        @pl.when(last)
        def _():
            for t in range(3):
                wait_send(hk.at[0], p2_s.at[s, t])
                wait_send(hk.at[0], p2e_s.at[s, t + 1])

        @pl.when(jnp.logical_not(last))
        def _():
            wait_send(hk.at[0, :, pl.ds(0, TB), :], p1_s.at[s, 0])
            for d in range(1, 3):
                wait_send(hk.at[0], p2_s.at[s, d])

        return carry

    lax.fori_loop(0, NZ, left, 0)

    @pl.when(last)
    def _():
        for t in range(3):
            n = 3 if t < 2 else 2
            wait_send(hq.at[pl.ds(0, n)], bq_s.at[t])
            wait_send(hx.at[pl.ds(0, n)], bx_s.at[t])
            wait_send(hq.at[:, pl.ds(0, TB), :], r1_s.at[t])

    @pl.when(jnp.logical_not(last))
    def _():
        wait_send(hq.at[:, pl.ds(0, TB), :], pq_s.at[0])
        wait_send(zx, px_s.at[0])
        for d in range(1, 4):
            wait_send(hq.at[:, pl.ds(0, TB), :], r1_s.at[d])

        @pl.when(y < 2)
        def _():
            for i in range(4):
                wait_send(hq.at[pl.ds(0, 3), pl.ds(0, TB), :], rb_s.at[i])

        @pl.when(y == 2)
        def _():
            for i in range(4):
                wait_send(hq.at[pl.ds(0, 2), pl.ds(0, TB), :], rb_s.at[i])

    for s in range(1, NZ):
        wait_send(ox.at[0], r2_s.at[s])
    for i in range(NZ):
        copy_wait(ox.at[0], r2_r.at[i])


def on_device(query_src, key_src, value_src, value_edit, tile_mask, word_map, blend_table):
    words, heads = blend_table.shape
    half = lax.axis_index("head") // 2
    mask_row = lax.dynamic_index_in_dim(tile_mask, half, 0, keepdims=False)
    bias = jnp.where(mask_row == 1, 0.0, MASKED).astype(jnp.float32)
    onehot = (jnp.arange(words, dtype=jnp.int32)[:, None] == word_map[None, :]).astype(jnp.float32)
    shares = lax.dot_general(
        blend_table, onehot, (((0,), (0,)), ((), ())), precision=lax.Precision.HIGHEST
    )
    shares = jnp.pad(shares.reshape(NZ, HZ, TB), ((0, 0), (0, 0), (0, 128 - TB)))
    ext = jnp.concatenate(
        [jnp.broadcast_to(bias, (NZ, 1, 128)), shares, jnp.zeros((NZ, 2, 128), jnp.float32)], axis=1
    )
    bf, f32 = jnp.bfloat16, jnp.float32
    dma = pltpu.SemaphoreType.DMA
    anywhere = pl.BlockSpec(memory_space=pl.ANY)
    vmem = pl.BlockSpec(memory_space=pltpu.VMEM)
    return pl.pallas_call(
        body,
        out_shape=jax.ShapeDtypeStruct(query_src.shape, bf),
        in_specs=[anywhere] * 4 + [vmem],
        out_specs=anywhere,
        scratch_shapes=[
            pltpu.VMEM((NZ, TB, HZ * HD), bf),
            pltpu.VMEM((NZ, 8, 128), f32),
            pltpu.VMEM((NZ, 3, TB, HZ * HD), bf),
            pltpu.VMEM((NZ, 128, HD), bf),
            pltpu.VMEM((NZ, 4, 8, 128), f32),
            pltpu.VMEM((NZ, 3, 128, HD), bf),
            pltpu.VMEM((SLOTS, 128, HD), bf),
            pltpu.VMEM((SLOTS, 4, 8, 128), f32),
            pltpu.VMEM((NZ, 3, NC, 4, 128, HD), bf),
            pltpu.VMEM((NZ, CK, HD), bf),
            pltpu.VMEM((ROWS, 2 * HD), bf),
            pltpu.VMEM((ROWS, 128), f32),
            pltpu.VMEM((ROWS, 128), f32),
            pltpu.VMEM((ROWS, 128), f32),
            pltpu.VMEM((ROWS, 2 * HD), f32),
            pltpu.VMEM((SLOTS, 128, HD), bf),
            pltpu.VMEM((NZ, TB, HZ * HD), bf),
            dma((NZ,)), dma((NZ,)), dma((NZ,)), dma((NZ,)), dma((NZ,)), dma((NZ,)),
            dma((4,)), dma((4,)), dma((4,)), dma((4,)), dma((4,)), dma((4,)),
            dma((3,)), dma(()), dma((3,)), dma(()),
            dma((NZ, 4)), dma((NZ, 4)), dma((NZ, 4)),
            dma((NZ, 3)), dma((NZ, 4)), dma((NZ, 4)), dma((NZ,)), dma((NZ,)),
            dma((4,)), dma((4,)), dma((4,)), dma((4, 3)), dma((1,)), dma(()),
            dma((NZ,)), dma((NZ,)),
        ],
        compiler_params=pltpu.CompilerParams(
            collective_id=0, has_side_effects=True, vmem_limit_bytes=48 * 1024 * 1024
        ),
        cost_estimate=pl.CostEstimate(
            flops=4 * ROWS * 8192 * 256, bytes_accessed=8 * 1024 * 1024, transcendentals=ROWS * 8192
        ),
    )(query_src, key_src, value_src, value_edit, ext)


def solution(mesh):
    return jax.shard_map(
        on_device,
        mesh=mesh,
        in_specs=(
            P(("seq", "head"), None),
            P(("seq", "head"), None),
            P(("seq", "head"), None),
            P(("seq", "head"), None),
            P("seq", None),
            P(("seq", "head")),
            P(),
        ),
        out_specs=P(("seq", "head"), None),
        check_vma=False,
    )
```

```python
import jax
import jax.numpy as jnp
from jax import lax
from jax.experimental import pallas as pl
from jax.experimental.pallas import tpu as pltpu
from jax.sharding import PartitionSpec as P

MESH = pl.DeviceIdType.MESH
HD = 128
NX, NY, NZ, NC = 4, 4, 8, 2
HZ = 5
TB = 32
SLOTS = 11
ROWS = SLOTS * 4 * TB
CK = 1024
QC = 704
MASKED = -(2.0**100)
OFFS = (0, 1, -1, 2, -2, 3, -3, 4)
VMEM_LIMIT = 60 * 1024 * 1024
LAGS = (0, 2, 4, 6)
READY = 8
AHEAD = 7
LOG2E = 1.4426950408889634


def offset_of(s):
    half = (s + 1) // 2
    return half * (2 * (s % 2) - 1)


def copy_wait(ref, sem):
    pltpu.make_async_copy(ref, ref, sem).wait()


def body(
    q_ref, k_ref, v_ref, w_ref, mask_ref, word_ref, blend_ref, out_ref,
    ext_ref, zq, zx, zkv, hq, hx, hk, ek, fk, qb, xb, kv, oh, qa, mix, mm, ll, oo, ro, ox,
    zq_s, zq_r, zx_s, zx_r, zk_s, zk_r,
    pq_s, pq_r, pqe_r, px_s, px_r, pxe_r, bq_s, bq_r, bx_s, bx_r,
    p1_s, p1_r, p1e_r, p1e_s, p2_s, p2_r, e_s, e_r, f_r, p3_s, h_r, c_s, c_r,
    r1_s, r1_r, rb_s, rb_r, re_s, re_r, r2_s, r2_r,
):
    seq = lax.axis_index("seq")
    head = lax.axis_index("head")
    z = (seq // 8) * 2 + head // 4
    x = (seq // 2) % 4
    c = seq % 2
    y = head % 4
    last = y == 3
    even = y % 2 == 0
    slot = (y % 2) * 2 + y // 2

    def dev(dx, dy, dz, dc):
        return ((dz // 2) * 8 + dx * 2 + dc, (dz % 2) * 4 + dy)

    def send(src, dst, ss, rs, to):
        pltpu.make_async_remote_copy(
            src_ref=src, dst_ref=dst, send_sem=ss, recv_sem=rs, device_id=to, device_id_type=MESH
        ).start()

    def local(src, dst, rs):
        pltpu.make_async_copy(src, dst, rs).start()

    def wait_send(src, ss):
        copy_wait(src, ss)

    def cols(ref3, zz, count):
        return ref3.at[:, pl.ds(pl.multiple_of(zz * (HZ * HD), HD), count * HD)]

    def lanes(j):
        return pl.ds(pl.multiple_of(j * HD, HD), HD)

    def block(i):
        return pl.ds(pl.multiple_of(i * TB, TB), TB)

    barrier = pltpu.get_barrier_semaphore()
    for d in range(1, NZ):
        pl.semaphore_signal(barrier, inc=1, device_id=dev(x, y, (z + d) % NZ, c), device_id_type=MESH)
    for d in range(1, NX * NY):
        pl.semaphore_signal(
            barrier, inc=1, device_id=dev((x + d // 4) % 4, (y + d % 4) % 4, z, c), device_id_type=MESH
        )
    pl.semaphore_signal(barrier, inc=1, device_id=dev(x, y, z, 1 - c), device_id_type=MESH)

    words = blend_ref.shape[1]
    hit = lax.broadcasted_iota(jnp.int32, (words, TB), 0) == word_ref[...]
    shares = jnp.dot(
        blend_ref[...], hit.astype(jnp.float32),
        precision=lax.Precision.HIGHEST, preferred_element_type=jnp.float32,
    )
    mask_row = jnp.where(mask_ref[pl.ds(head // 2, 1), :] == 1, 0.0, MASKED).astype(jnp.float32)
    for i in range(NZ):
        ext_ref[i] = jnp.zeros((8, 128), jnp.float32)
        ext_ref[i, 0:1, :] = mask_row
        ext_ref[i, 1 : 1 + HZ, 0:TB] = shares[i * HZ : (i + 1) * HZ, :]
    row = lax.broadcasted_iota(jnp.int32, (CK, HD), 0)
    lane = lax.broadcasted_iota(jnp.int32, (CK, HD), 1)
    tile = (row // TB) % 4 * 8 + (row // 512) * 4 + (row // 128) % 2

    def fill_onehot(zz, carry):
        base = (zz // 2) * 32 + (zz % 2) * 2
        oh[zz] = jnp.where(lane - base == tile, 1.0, 0.0).astype(jnp.bfloat16)
        return carry

    lax.fori_loop(0, NZ, fill_onehot, 0)
    mm[...] = jnp.full(mm.shape, MASKED, jnp.float32)
    ll[...] = jnp.zeros(ll.shape, jnp.float32)

    def clear(i, carry):
        oo[pl.ds(pl.multiple_of(i * 128, 128), 128), :] = jnp.zeros((128, 2 * HD), jnp.float32)
        return carry

    lax.fori_loop(0, SLOTS, clear, 0)

    @pl.when(y >= 2)
    def _():
        qb[10] = jnp.zeros(qb.shape[1:], qb.dtype)
        xb[10] = jnp.zeros(xb.shape[1:], xb.dtype)

    @pl.when(last)
    def _():
        qb[8:10] = jnp.zeros((2,) + qb.shape[1:], qb.dtype)
        xb[8:10] = jnp.zeros((2,) + xb.shape[1:], xb.dtype)

    pl.semaphore_wait(barrier, NZ + NX * NY - 1)

    local(cols(q_ref, z, HZ), zq.at[z], zq_r.at[z])
    local(ext_ref.at[z], zx.at[z], zx_r.at[z])
    for s in range(1, NZ):
        to = (z - OFFS[s] + NZ) % NZ
        send(cols(q_ref, to, HZ), zq.at[z], zq_s.at[s], zq_r.at[z], dev(x, y, to, c))
        send(ext_ref.at[to], zx.at[z], zx_s.at[s], zx_r.at[z], dev(x, y, to, c))
    for i, ref in enumerate((k_ref, v_ref, w_ref)):
        local(cols(ref, z, HZ), zkv.at[z, i], zk_r.at[z])

    def stage_zero(s):
        to = (z - offset_of(s) + NZ) % NZ
        for i, ref in enumerate((k_ref, v_ref, w_ref)):
            send(cols(ref, to, HZ), zkv.at[z, i], zk_s.at[s], zk_r.at[z], dev(x, y, to, c))

    for s in range(1, 1 + AHEAD):
        stage_zero(s)

    def spread_queries():
        for i in range(NZ):
            copy_wait(zq.at[i], zq_r.at[i])
            copy_wait(zx.at[i], zx_r.at[i])

        def to_lines(qdst, xdst):
            local(zq.at[:, :, lanes(x)], qdst, pq_r.at[x])
            local(zx, xdst, px_r.at[x])
            for d in range(1, 4):
                j = (x + d) % 4
                send(zq.at[:, :, lanes(j)], qdst, pq_s.at[d], pq_r.at[x], dev(j, y, z, c))
                send(zx, xdst, px_s.at[d], px_r.at[x], dev(j, y, z, c))

        @pl.when(last)
        def _():
            to_lines(hq.at[:, block(x), :], hx.at[:, x])
            local(zq.at[:, :, pl.ds(4 * HD, HD)], qb.at[pl.ds(0, 8), pl.ds(3 * TB, TB), :], pqe_r.at[3])
            local(zx, xb.at[pl.ds(0, 8), 3], pxe_r.at[3])

        @pl.when(jnp.logical_not(last))
        def _():
            to_lines(qb.at[pl.ds(0, 8), block(x), :], xb.at[pl.ds(0, 8), x])
            send(
                zq.at[:, :, pl.ds(4 * HD, HD)], qb.at[pl.ds(0, 8), block(y), :],
                pq_s.at[0], pqe_r.at[y], dev(x, 3, z, c),
            )
            send(zx, xb.at[pl.ds(0, 8), y], px_s.at[0], pxe_r.at[y], dev(x, 3, z, c))

    def lend_queries():
        for i in range(4):
            copy_wait(hq.at[:, pl.ds(0, TB), :], pq_r.at[i])
            copy_wait(zx, px_r.at[i])

        @pl.when(last)
        def _():
            for t in range(3):
                n = 3 if t < 2 else 2
                send(hq.at[pl.ds(3 * t, n)], qb.at[pl.ds(8, n)], bq_s.at[t], bq_r, dev(x, t, z, c))
                send(hx.at[pl.ds(3 * t, n)], xb.at[pl.ds(8, n)], bx_s.at[t], bx_r, dev(x, t, z, c))
            for i in range(4):
                copy_wait(hq.at[:, pl.ds(0, TB), :], pqe_r.at[i])
                copy_wait(zx, pxe_r.at[i])

    def ready_queries():
        @pl.when(y < 2)
        def _():
            copy_wait(qb.at[pl.ds(8, 3)], bq_r)
            copy_wait(xb.at[pl.ds(8, 3)], bx_r)

        @pl.when(y == 2)
        def _():
            copy_wait(qb.at[pl.ds(8, 2)], bq_r)
            copy_wait(xb.at[pl.ds(8, 2)], bx_r)

        which = 1 + jnp.where(last, 4, x)
        sub = lax.broadcasted_iota(jnp.int32, (4, 8, 128), 1)
        diag = lax.broadcasted_iota(jnp.int32, (4, TB, 128), 1) == lax.broadcasted_iota(
            jnp.int32, (4, TB, 128), 2
        )

        def one(i, carry):
            rows = pl.ds(pl.multiple_of(i * 128, 128), 128)
            extra = xb[i]
            qa[rows, 0:HD] = qb[i]
            bias = jnp.broadcast_to(extra[:, 0:1, :], (4, TB, 128))
            qa[rows, HD : 2 * HD] = bias.reshape(128, 128).astype(jnp.bfloat16)
            shares = jnp.sum(jnp.where(sub == which, extra, 0.0), axis=1, keepdims=True)
            column = jnp.sum(jnp.where(diag, shares, 0.0), axis=2, keepdims=True)
            mix[rows, :] = jnp.broadcast_to(column, (4, TB, 128)).reshape(128, 128)
            return carry

        lax.fori_loop(0, SLOTS, one, 0)

    def source(s):
        return (z + offset_of(s) + NZ) % NZ

    def stage_one(s):
        zz = source(s)
        copy_wait(zkv.at[zz], zk_r.at[zz])

        def to_lines(dst):
            local(zkv.at[zz, :, :, lanes(x)], dst, p1_r.at[s, x])
            for d in range(1, 4):
                j = (x + d) % 4
                send(zkv.at[zz, :, :, lanes(j)], dst, p1_s.at[s, d], p1_r.at[s, x], dev(j, y, z, c))

        if AHEAD < 7:

            @pl.when(jnp.logical_and(s >= 1, s + AHEAD < NZ))
            def _():
                stage_zero(s + AHEAD)

        fifth = zkv.at[zz, :, :, pl.ds(4 * HD, HD)]

        @pl.when(last)
        def _():
            to_lines(hk.at[zz, :, block(x), :])
            local(fifth, kv.at[zz, :, c, 3, block(x), :], p1e_r.at[s, 3])

        @pl.when(jnp.logical_not(last))
        def _():
            to_lines(kv.at[zz, :, c, slot, block(x), :])

        @pl.when(y == 1)
        def _():
            send(fifth, kv.at[zz, :, c, 2, block(x), :], p1_s.at[s, 0], p1e_r.at[s, 2], dev(x, 3, z, c))

        @pl.when(even)
        def _():
            local(fifth, ek.at[zz, :, block(x), :], p1e_r.at[s, x])
            for d in range(1, 4):
                send(
                    fifth, ek.at[zz, :, block(x), :], p1e_s.at[s, d], p1e_r.at[s, x],
                    dev((x + d) % 4, y, z, c),
                )

    low, high = pl.ds(0, 2 * TB), pl.ds(2 * TB, 2 * TB)

    def stage_two(s):
        zz = source(s)
        piece = hk.at[zz, :, pl.ds(0, TB), :]
        for i in range(4):
            copy_wait(piece, p1_r.at[s, i])
        own = kv.at[zz, :, c, slot]

        @pl.when(last)
        def _():
            send(hk.at[zz], own, p2_s.at[s, 0], p2_r.at[s, 3], dev(x, 0, z, c))
            send(hk.at[zz], own, p2_s.at[s, 1], p2_r.at[s, 3], dev(x, 2, z, c))
            copy_wait(piece, p1e_r.at[s, 2])
            copy_wait(piece, p1e_r.at[s, 3])
            mine = kv.at[zz, :, c, pl.ds(2, 2), block(x), :]
            for d in range(1, 4):
                send(mine, mine, e_s.at[s, d], e_r.at[s, x], dev((x + d) % 4, 3, z, c))

        @pl.when(y == 1)
        def _():
            send(own, own, p2_s.at[s, 0], p2_r.at[s, slot], dev(x, 0, z, c))
            send(own, own, p2_s.at[s, 1], p2_r.at[s, slot], dev(x, 2, z, c))

        @pl.when(even)
        def _():
            send(own, own, p2_s.at[s, 0], p2_r.at[s, slot], dev(x, 1, z, c))
            send(
                kv.at[zz, :, c, slot, high, :], fk.at[zz, slot], p2_s.at[s, 1], f_r.at[s, slot],
                dev(x, 3, z, c),
            )
            for i in range(4):
                copy_wait(piece, p1e_r.at[s, i])
            send(ek.at[zz], own, e_s.at[s, 0], p2_r.at[s, slot], dev(x, 3, z, c))

    def stage_relay(s):
        zz = source(s)

        def part(who, rows):
            return kv.at[zz, :, c, who, rows, :]

        @pl.when(last)
        def _():
            for i in range(2):
                copy_wait(fk.at[zz, i], f_r.at[s, i])
                send(fk.at[zz, i], part(i, high), p3_s.at[s, i], h_r.at[s, 1], dev(x, 2 - 2 * i, z, c))

        @pl.when(y == 1)
        def _():
            for i in range(2):
                copy_wait(hk.at[zz], p2_r.at[s, i])
                send(part(i, low), part(i, low), p3_s.at[s, i], h_r.at[s, 0], dev(x, 2 - 2 * i, z, c))

        @pl.when(y == 0)
        def _():
            copy_wait(hk.at[zz], p2_r.at[s, 2])
            copy_wait(hk.at[zz], p2_r.at[s, 3])
            send(part(3, low), part(3, low), p3_s.at[s, 0], h_r.at[s, 0], dev(x, 1, z, c))

        @pl.when(y == 2)
        def _():
            copy_wait(hk.at[zz], p2_r.at[s, 2])
            copy_wait(hk.at[zz], p2_r.at[s, 3])
            send(part(3, high), part(3, high), p3_s.at[s, 0], h_r.at[s, 1], dev(x, 1, z, c))

    def stage_three(s):
        zz = source(s)

        @pl.when(last)
        def _():
            for i in range(2):
                copy_wait(hk.at[zz], p2_r.at[s, i])
            for d in range(1, 4):
                copy_wait(kv.at[zz, :, 0, pl.ds(2, 2), pl.ds(0, TB), :], e_r.at[s, (x + d) % 4])

        @pl.when(jnp.logical_not(last))
        def _():
            for i in range(2):
                copy_wait(fk.at[zz, 0], h_r.at[s, i])

        half = kv.at[zz, :, c]
        send(half, half, c_s.at[s], c_r.at[s], dev(x, y, z, 1 - c))

    scale = HD ** (-0.5) * LOG2E

    def fold(parts, op):
        while len(parts) > 1:
            parts = [
                op(parts[i], parts[i + 1]) if i + 1 < len(parts) else parts[i]
                for i in range(0, len(parts), 2)
            ]
        return parts[0]

    def attend(s):
        zz = source(s)
        copy_wait(kv.at[zz, :, 0], c_r.at[s])

        def score(i):
            rows = pl.ds(i * QC, QC)
            tiles = []
            for k in range(0, CK, 256):
                keys = jnp.concatenate(
                    [kv[zz, 0].reshape(CK, HD)[k : k + 256], oh[zz, k : k + 256]], axis=1
                )
                scores = lax.dot_general(
                    qa[rows, :], keys, (((1,), (1,)), ((), ())), preferred_element_type=jnp.float32
                )
                tiles += [scores[:, :128], scores[:, 128:]]
            return tiles, jnp.max(fold(tiles, jnp.maximum), axis=1, keepdims=True)

        def gather(i, tiles, largest):
            rows = pl.ds(i * QC, QC)
            old = mm[rows, :]
            new = jnp.maximum(old, largest)
            weights = [jnp.exp2((t - new) * scale) for t in tiles]
            shrink = jnp.exp2((old - new) * scale)
            mm[rows, :] = new
            ll[rows, :] = ll[rows, :] * shrink + fold(weights, jnp.add)
            values = jnp.concatenate([kv[zz, 1].reshape(CK, HD), kv[zz, 2].reshape(CK, HD)], axis=1)
            low_weights = jnp.concatenate([w.astype(jnp.bfloat16) for w in weights], axis=1)
            sums = jnp.dot(low_weights, values, preferred_element_type=jnp.float32)
            oo[rows, :] = oo[rows, :] * jnp.concatenate([shrink, shrink], axis=1) + sums

        held = None
        for i in range(ROWS // QC):
            now = score(i)
            if held is not None:
                gather(i - 1, *held)
            held = now
        gather(ROWS // QC - 1, *held)

    def moves(t):
        for stage, lag in zip((stage_three, stage_relay, stage_two, stage_one), LAGS[::-1]):

            @pl.when(jnp.logical_and(t >= lag, t < NZ + lag))
            def _(stage=stage, lag=lag):
                stage(t - lag)

    def fill(t, carry):
        moves(t)

        @pl.when(t == 0)
        def _():
            spread_queries()

        @pl.when(t == 1)
        def _():
            lend_queries()

        @pl.when(t == 2)
        def _():
            ready_queries()

        return carry

    def step(t, carry):
        attend(t - READY)
        moves(t)
        return carry

    lax.fori_loop(0, READY, fill, 0)
    lax.fori_loop(READY, READY + NZ, step, 0)

    def finish(i, carry):
        rows = pl.ds(pl.multiple_of(i * 128, 128), 128)
        total = jnp.sum(ll[rows, :], axis=1, keepdims=True)
        share = mix[rows, :]
        both = oo[rows, :] / total
        ro[i] = (share * both[:, HD:] + (1.0 - share) * both[:, :HD]).astype(jnp.bfloat16)
        return carry

    lax.fori_loop(0, SLOTS, finish, 0)

    @pl.when(last)
    def _():
        e_lanes = pl.ds(4 * HD, HD)
        local(ro.at[pl.ds(0, 8), pl.ds(3 * TB, TB), :], ox.at[:, :, e_lanes], re_r)
        for t in range(3):
            send(ro.at[pl.ds(0, 8), pl.ds(t * TB, TB), :], ox.at[:, :, e_lanes], r1_s.at[t], re_r, dev(x, t, z, c))
        for j in range(4):
            for t in range(3):
                n = 3 if t < 2 else 2
                copy_wait(ox.at[pl.ds(3 * t, n), :, lanes(j)], rb_r.at[j, t])

    @pl.when(jnp.logical_not(last))
    def _():
        mine = lanes(x)
        local(ro.at[pl.ds(0, 8), block(x), :], ox.at[:, :, mine], r1_r.at[x])
        for d in range(1, 4):
            j = (x + d) % 4
            send(ro.at[pl.ds(0, 8), block(j), :], ox.at[:, :, mine], r1_s.at[d], r1_r.at[x], dev(j, y, z, c))
        for i in range(4):

            @pl.when(y < 2)
            def _():
                send(
                    ro.at[pl.ds(8, 3), pl.ds(i * TB, TB), :], ox.at[pl.ds(3 * y, 3), :, mine],
                    rb_s.at[i], rb_r.at[x, y], dev(i, 3, z, c),
                )

            @pl.when(y == 2)
            def _():
                send(
                    ro.at[pl.ds(8, 2), pl.ds(i * TB, TB), :], ox.at[pl.ds(6, 2), :, mine],
                    rb_s.at[i], rb_r.at[x, 2], dev(i, 3, z, c),
                )

        for i in range(4):
            copy_wait(ox.at[:, :, lanes(i)], r1_r.at[i])

    copy_wait(ox.at[:, :, pl.ds(4 * HD, HD)], re_r)
    target = cols(out_ref, z, HZ)
    local(ox.at[z], target, r2_r.at[z])
    for s in range(1, NZ):
        to = (z - OFFS[s] + NZ) % NZ
        send(ox.at[to], target, r2_s.at[s], r2_r.at[z], dev(x, y, to, c))

    for s in range(1, NZ):
        wait_send(zq.at[0], zq_s.at[s])
        wait_send(zx.at[0], zx_s.at[s])
        wait_send(zkv.at[0], zk_s.at[s])
    for d in range(1, 4):
        wait_send(hq.at[:, pl.ds(0, TB), :], pq_s.at[d])
        wait_send(zx, px_s.at[d])

    def left(s, carry):
        for d in range(1, 4):
            wait_send(hk.at[0, :, pl.ds(0, TB), :], p1_s.at[s, d])
        wait_send(kv.at[0, :, 0], c_s.at[s])

        wait_send(hk.at[0], p2_s.at[s, 0])
        wait_send(fk.at[0, 0], p3_s.at[s, 0])

        @pl.when(last)
        def _():
            for d in range(1, 4):
                wait_send(kv.at[0, :, 0, pl.ds(2, 2), pl.ds(0, TB), :], e_s.at[s, d])

        @pl.when(jnp.logical_not(even))
        def _():
            wait_send(hk.at[0], p2_s.at[s, 1])
            wait_send(fk.at[0, 0], p3_s.at[s, 1])

        @pl.when(y == 1)
        def _():
            wait_send(hk.at[0, :, pl.ds(0, TB), :], p1_s.at[s, 0])

        @pl.when(even)
        def _():
            wait_send(fk.at[0, 0], p2_s.at[s, 1])
            wait_send(hk.at[0], e_s.at[s, 0])
            for d in range(1, 4):
                wait_send(hk.at[0, :, pl.ds(0, TB), :], p1e_s.at[s, d])

        return carry

    lax.fori_loop(0, NZ, left, 0)

    @pl.when(last)
    def _():
        for t in range(3):
            n = 3 if t < 2 else 2
            wait_send(hq.at[pl.ds(0, n)], bq_s.at[t])
            wait_send(hx.at[pl.ds(0, n)], bx_s.at[t])
            wait_send(hq.at[:, pl.ds(0, TB), :], r1_s.at[t])

    @pl.when(jnp.logical_not(last))
    def _():
        wait_send(hq.at[:, pl.ds(0, TB), :], pq_s.at[0])
        wait_send(zx, px_s.at[0])
        for d in range(1, 4):
            wait_send(hq.at[:, pl.ds(0, TB), :], r1_s.at[d])

        @pl.when(y < 2)
        def _():
            for i in range(4):
                wait_send(hq.at[pl.ds(0, 3), pl.ds(0, TB), :], rb_s.at[i])

        @pl.when(y == 2)
        def _():
            for i in range(4):
                wait_send(hq.at[pl.ds(0, 2), pl.ds(0, TB), :], rb_s.at[i])

    for s in range(1, NZ):
        wait_send(ox.at[0], r2_s.at[s])
    for i in range(NZ):
        copy_wait(ox.at[0], r2_r.at[i])


def on_device(query_src, key_src, value_src, value_edit, tile_mask, word_map, blend_table):
    bf, f32 = jnp.bfloat16, jnp.float32
    dma = pltpu.SemaphoreType.DMA
    anywhere = pl.BlockSpec(memory_space=pl.ANY)
    vmem = pl.BlockSpec(memory_space=pltpu.VMEM)
    return pl.pallas_call(
        body,
        out_shape=jax.ShapeDtypeStruct(query_src.shape, bf),
        in_specs=[anywhere] * 4 + [vmem] * 3,
        out_specs=vmem,
        scratch_shapes=[
            pltpu.VMEM((NZ, 8, 128), f32),
            pltpu.VMEM((NZ, TB, HZ * HD), bf),
            pltpu.VMEM((NZ, 8, 128), f32),
            pltpu.VMEM((NZ, 3, TB, HZ * HD), bf),
            pltpu.VMEM((NZ, 128, HD), bf),
            pltpu.VMEM((NZ, 4, 8, 128), f32),
            pltpu.VMEM((NZ, 3, 128, HD), bf),
            pltpu.VMEM((NZ, 3, 128, HD), bf),
            pltpu.VMEM((NZ, 2, 3, 2 * TB, HD), bf),
            pltpu.VMEM((SLOTS, 128, HD), bf),
            pltpu.VMEM((SLOTS, 4, 8, 128), f32),
            pltpu.VMEM((NZ, 3, NC, 4, 128, HD), bf),
            pltpu.VMEM((NZ, CK, HD), bf),
            pltpu.VMEM((ROWS, 2 * HD), bf),
            pltpu.VMEM((ROWS, 128), f32),
            pltpu.VMEM((ROWS, 128), f32),
            pltpu.VMEM((ROWS, 128), f32),
            pltpu.VMEM((ROWS, 2 * HD), f32),
            pltpu.VMEM((SLOTS, 128, HD), bf),
            pltpu.VMEM((NZ, TB, HZ * HD), bf),
            dma((NZ,)), dma((NZ,)), dma((NZ,)), dma((NZ,)), dma((NZ,)), dma((NZ,)),
            dma((4,)), dma((4,)), dma((4,)), dma((4,)), dma((4,)), dma((4,)),
            dma((3,)), dma(()), dma((3,)), dma(()),
            dma((NZ, 4)), dma((NZ, 4)), dma((NZ, 4)),
            dma((NZ, 4)), dma((NZ, 2)), dma((NZ, 4)), dma((NZ, 4)), dma((NZ, 4)),
            dma((NZ, 2)), dma((NZ, 2)), dma((NZ, 2)), dma((NZ,)), dma((NZ,)),
            dma((4,)), dma((4,)), dma((4,)), dma((4, 3)), dma((1,)), dma(()),
            dma((NZ,)), dma((NZ,)),
        ],
        compiler_params=pltpu.CompilerParams(
            collective_id=0, has_side_effects=True, vmem_limit_bytes=VMEM_LIMIT
        ),
        cost_estimate=pl.CostEstimate(
            flops=4 * ROWS * 8192 * 256, bytes_accessed=8 * 1024 * 1024, transcendentals=ROWS * 8192
        ),
    )(query_src, key_src, value_src, value_edit, tile_mask, word_map.reshape(1, TB), blend_table.T)


def solution(mesh):
    return jax.shard_map(
        on_device,
        mesh=mesh,
        in_specs=(
            P(("seq", "head"), None),
            P(("seq", "head"), None),
            P(("seq", "head"), None),
            P(("seq", "head"), None),
            P("seq", None),
            P(("seq", "head")),
            P(),
        ),
        out_specs=P(("seq", "head"), None),
        check_vma=False,
    )
```

```python
import jax
import jax.numpy as jnp
from jax import lax
from jax.experimental import pallas as pl
from jax.experimental.pallas import tpu as pltpu
from jax.sharding import PartitionSpec as P

MESH = pl.DeviceIdType.MESH
HD = 128
NX, NY, NZ, NC = 4, 4, 8, 2
HZ = 5
TB = 32
SLOTS = 11
ROWS = SLOTS * 4 * TB
CK = 1024
QC = 704
MASKED = -(2.0**100)
OFFS = (0, 1, -1, 2, -2, 3, -3, 4)
VMEM_LIMIT = 60 * 1024 * 1024
LEADS = (1, 3, 5)
AHEAD = 7
LOG2E = 1.4426950408889634


def offset_of(s):
    half = (s + 1) // 2
    return half * (2 * (s % 2) - 1)


def copy_wait(ref, sem):
    pltpu.make_async_copy(ref, ref, sem).wait()


def body(
    q_ref, k_ref, v_ref, w_ref, mask_ref, word_ref, blend_ref, out_ref,
    ext_ref, zq, zx, zkv, hq, hx, hk, ek, qb, xb, kv, oh, qa, mix, mm, ll, oo, ro, ox,
    zq_s, zq_r, zx_s, zx_r, zk_s, zk_r,
    pq_s, pq_r, pqe_r, px_s, px_r, pxe_r, bq_s, bq_r, bx_s, bx_r,
    p1_s, p1_r, p1e_r, p1e_s, p2_s, p2_r, e_s, e_r, c_s, c_r,
    r1_s, r1_r, rb_s, rb_r, re_r, r2_s, r2_r,
):
    seq = lax.axis_index("seq")
    head = lax.axis_index("head")
    z = (seq // 8) * 2 + head // 4
    x = (seq // 2) % 4
    c = seq % 2
    y = head % 4
    last = y == 3
    even = y % 2 == 0
    slot = (y % 2) * 2 + y // 2

    def dev(dx, dy, dz, dc):
        return ((dz // 2) * 8 + dx * 2 + dc, (dz % 2) * 4 + dy)

    def send(src, dst, ss, rs, to):
        pltpu.make_async_remote_copy(
            src_ref=src, dst_ref=dst, send_sem=ss, recv_sem=rs, device_id=to, device_id_type=MESH
        ).start()

    def local(src, dst, rs):
        pltpu.make_async_copy(src, dst, rs).start()

    def wait_send(src, ss):
        copy_wait(src, ss)

    def cols(ref3, zz, count):
        return ref3.at[:, pl.ds(pl.multiple_of(zz * (HZ * HD), HD), count * HD)]

    def lanes(j):
        return pl.ds(pl.multiple_of(j * HD, HD), HD)

    def block(i):
        return pl.ds(pl.multiple_of(i * TB, TB), TB)

    barrier = pltpu.get_barrier_semaphore()
    for d in range(1, NZ):
        pl.semaphore_signal(barrier, inc=1, device_id=dev(x, y, (z + d) % NZ, c), device_id_type=MESH)
    for d in range(1, NX * NY):
        pl.semaphore_signal(
            barrier, inc=1, device_id=dev((x + d // 4) % 4, (y + d % 4) % 4, z, c), device_id_type=MESH
        )
    pl.semaphore_signal(barrier, inc=1, device_id=dev(x, y, z, 1 - c), device_id_type=MESH)

    words = blend_ref.shape[1]
    hit = lax.broadcasted_iota(jnp.int32, (words, TB), 0) == word_ref[...]
    shares = jnp.dot(
        blend_ref[...], hit.astype(jnp.float32),
        precision=lax.Precision.HIGHEST, preferred_element_type=jnp.float32,
    )
    mask_row = jnp.where(mask_ref[pl.ds(head // 2, 1), :] == 1, 0.0, MASKED).astype(jnp.float32)
    for i in range(NZ):
        ext_ref[i] = jnp.zeros((8, 128), jnp.float32)
        ext_ref[i, 0:1, :] = mask_row
        ext_ref[i, 1 : 1 + HZ, 0:TB] = shares[i * HZ : (i + 1) * HZ, :]
    row = lax.broadcasted_iota(jnp.int32, (CK, HD), 0)
    lane = lax.broadcasted_iota(jnp.int32, (CK, HD), 1)
    tile = (row // TB) % 4 * 8 + (row // 512) * 4 + (row // 128) % 2

    def fill_onehot(zz, carry):
        base = (zz // 2) * 32 + (zz % 2) * 2
        oh[zz] = jnp.where(lane - base == tile, 1.0, 0.0).astype(jnp.bfloat16)
        return carry

    lax.fori_loop(0, NZ, fill_onehot, 0)
    mm[...] = jnp.full(mm.shape, MASKED, jnp.float32)
    ll[...] = jnp.zeros(ll.shape, jnp.float32)

    def clear(i, carry):
        oo[pl.ds(pl.multiple_of(i * 128, 128), 128), :] = jnp.zeros((128, 2 * HD), jnp.float32)
        return carry

    lax.fori_loop(0, SLOTS, clear, 0)

    @pl.when(y >= 2)
    def _():
        qb[10] = jnp.zeros(qb.shape[1:], qb.dtype)
        xb[10] = jnp.zeros(xb.shape[1:], xb.dtype)

    @pl.when(last)
    def _():
        qb[8:10] = jnp.zeros((2,) + qb.shape[1:], qb.dtype)
        xb[8:10] = jnp.zeros((2,) + xb.shape[1:], xb.dtype)

    pl.semaphore_wait(barrier, NZ + NX * NY - 1)

    local(cols(q_ref, z, HZ), zq.at[z], zq_r.at[z])
    local(ext_ref.at[z], zx.at[z], zx_r.at[z])
    for s in range(1, NZ):
        to = (z - OFFS[s] + NZ) % NZ
        send(cols(q_ref, to, HZ), zq.at[z], zq_s.at[s], zq_r.at[z], dev(x, y, to, c))
        send(ext_ref.at[to], zx.at[z], zx_s.at[s], zx_r.at[z], dev(x, y, to, c))
    for i, ref in enumerate((k_ref, v_ref, w_ref)):
        local(cols(ref, z, HZ), zkv.at[z, i], zk_r.at[z])

    def stage_zero(s):
        to = (z - (OFFS[s] if isinstance(s, int) else offset_of(s)) + NZ) % NZ
        for i, ref in enumerate((k_ref, v_ref, w_ref)):
            send(cols(ref, to, HZ), zkv.at[z, i], zk_s.at[s], zk_r.at[z], dev(x, y, to, c))

    for s in range(1, 1 + AHEAD):
        stage_zero(s)

    def spread_queries():
        for i in range(NZ):
            copy_wait(zq.at[i], zq_r.at[i])
            copy_wait(zx.at[i], zx_r.at[i])

        def to_lines(qdst, xdst):
            local(zq.at[:, :, lanes(x)], qdst, pq_r.at[x])
            local(zx, xdst, px_r.at[x])
            for d in range(1, 4):
                j = (x + d) % 4
                send(zq.at[:, :, lanes(j)], qdst, pq_s.at[d], pq_r.at[x], dev(j, y, z, c))
                send(zx, xdst, px_s.at[d], px_r.at[x], dev(j, y, z, c))

        @pl.when(last)
        def _():
            to_lines(hq.at[:, block(x), :], hx.at[:, x])
            local(zq.at[:, :, pl.ds(4 * HD, HD)], qb.at[pl.ds(0, 8), pl.ds(3 * TB, TB), :], pqe_r.at[3])
            local(zx, xb.at[pl.ds(0, 8), 3], pxe_r.at[3])

        @pl.when(jnp.logical_not(last))
        def _():
            to_lines(qb.at[pl.ds(0, 8), block(x), :], xb.at[pl.ds(0, 8), x])
            send(
                zq.at[:, :, pl.ds(4 * HD, HD)], qb.at[pl.ds(0, 8), block(y), :],
                pq_s.at[0], pqe_r.at[y], dev(x, 3, z, c),
            )
            send(zx, xb.at[pl.ds(0, 8), y], px_s.at[0], pxe_r.at[y], dev(x, 3, z, c))

    def lend_queries():
        for i in range(4):
            copy_wait(hq.at[:, pl.ds(0, TB), :], pq_r.at[i])
            copy_wait(zx, px_r.at[i])

        @pl.when(last)
        def _():
            for t in range(3):
                n = 3 if t < 2 else 2
                send(hq.at[pl.ds(3 * t, n)], qb.at[pl.ds(8, n)], bq_s.at[t], bq_r, dev(x, t, z, c))
                send(hx.at[pl.ds(3 * t, n)], xb.at[pl.ds(8, n)], bx_s.at[t], bx_r, dev(x, t, z, c))
            for i in range(4):
                copy_wait(hq.at[:, pl.ds(0, TB), :], pqe_r.at[i])
                copy_wait(zx, pxe_r.at[i])

    def ready_queries():
        @pl.when(y < 2)
        def _():
            copy_wait(qb.at[pl.ds(8, 3)], bq_r)
            copy_wait(xb.at[pl.ds(8, 3)], bx_r)

        @pl.when(y == 2)
        def _():
            copy_wait(qb.at[pl.ds(8, 2)], bq_r)
            copy_wait(xb.at[pl.ds(8, 2)], bx_r)

        which = 1 + jnp.where(last, 4, x)
        sub = lax.broadcasted_iota(jnp.int32, (4, 8, 128), 1)
        diag = lax.broadcasted_iota(jnp.int32, (4, TB, 128), 1) == lax.broadcasted_iota(
            jnp.int32, (4, TB, 128), 2
        )

        def one(i, carry):
            rows = pl.ds(pl.multiple_of(i * 128, 128), 128)
            extra = xb[i]
            qa[rows, 0:HD] = qb[i]
            bias = jnp.broadcast_to(extra[:, 0:1, :], (4, TB, 128))
            qa[rows, HD : 2 * HD] = bias.reshape(128, 128).astype(jnp.bfloat16)
            shares = jnp.sum(jnp.where(sub == which, extra, 0.0), axis=1, keepdims=True)
            column = jnp.sum(jnp.where(diag, shares, 0.0), axis=2, keepdims=True)
            mix[rows, :] = jnp.broadcast_to(column, (4, TB, 128)).reshape(128, 128)
            return carry

        lax.fori_loop(0, SLOTS, one, 0)

    def source(s):
        return (z + (OFFS[s] if isinstance(s, int) else offset_of(s)) + NZ) % NZ

    def stage_one(s):
        zz = source(s)
        copy_wait(zkv.at[zz], zk_r.at[zz])

        def to_lines(dst):
            local(zkv.at[zz, :, :, lanes(x)], dst, p1_r.at[s, x])
            for d in range(1, 4):
                j = (x + d) % 4
                send(zkv.at[zz, :, :, lanes(j)], dst, p1_s.at[s, d], p1_r.at[s, x], dev(j, y, z, c))

        if AHEAD < 7:

            @pl.when(jnp.logical_and(s >= 1, s + AHEAD < NZ))
            def _():
                stage_zero(s + AHEAD)

        fifth = zkv.at[zz, :, :, pl.ds(4 * HD, HD)]

        @pl.when(last)
        def _():
            to_lines(hk.at[zz, :, block(x), :])
            local(fifth, kv.at[zz, :, c, 3, block(x), :], p1e_r.at[s, 3])

        @pl.when(jnp.logical_not(last))
        def _():
            to_lines(kv.at[zz, :, c, slot, block(x), :])

        @pl.when(y == 1)
        def _():
            send(fifth, kv.at[zz, :, c, 2, block(x), :], p1_s.at[s, 0], p1e_r.at[s, 2], dev(x, 3, z, c))

        @pl.when(even)
        def _():
            local(fifth, ek.at[zz, :, block(x), :], p1e_r.at[s, x])
            for d in range(1, 4):
                send(
                    fifth, ek.at[zz, :, block(x), :], p1e_s.at[s, d], p1e_r.at[s, x],
                    dev((x + d) % 4, y, z, c),
                )

    def stage_two(s):
        zz = source(s)
        piece = hk.at[zz, :, pl.ds(0, TB), :]
        for i in range(4):
            copy_wait(piece, p1_r.at[s, i])
        own = kv.at[zz, :, c, slot]

        @pl.when(last)
        def _():
            send(hk.at[zz], own, p2_s.at[s, 0], p2_r.at[s, 3], dev(x, 0, z, c))
            send(hk.at[zz], own, p2_s.at[s, 1], p2_r.at[s, 3], dev(x, 2, z, c))
            send(hk.at[zz], own, p2_s.at[s, 2], p2_r.at[s, 3], dev(x, 1, z, c))
            copy_wait(piece, p1e_r.at[s, 2])
            copy_wait(piece, p1e_r.at[s, 3])
            mine = kv.at[zz, :, c, pl.ds(2, 2), block(x), :]
            for d in range(1, 4):
                send(mine, mine, e_s.at[s, d], e_r.at[s, x], dev((x + d) % 4, 3, z, c))

        @pl.when(y == 1)
        def _():
            send(own, own, p2_s.at[s, 0], p2_r.at[s, slot], dev(x, 0, z, c))
            send(own, own, p2_s.at[s, 1], p2_r.at[s, slot], dev(x, 2, z, c))

        @pl.when(even)
        def _():
            send(own, own, p2_s.at[s, 0], p2_r.at[s, slot], dev(x, 1, z, c))
            send(own, own, p2_s.at[s, 1], p2_r.at[s, slot], dev(x, 2 - y, z, c))
            for i in range(4):
                copy_wait(piece, p1e_r.at[s, i])
            send(ek.at[zz], own, e_s.at[s, 0], p2_r.at[s, slot], dev(x, 3, z, c))

    def stage_three(s):
        zz = source(s)

        @pl.when(last)
        def _():
            for i in range(2):
                copy_wait(hk.at[zz], p2_r.at[s, i])
            for d in range(1, 4):
                copy_wait(kv.at[zz, :, 0, pl.ds(2, 2), pl.ds(0, TB), :], e_r.at[s, (x + d) % 4])

        @pl.when(jnp.logical_not(last))
        def _():
            for d in range(1, 4):
                copy_wait(hk.at[zz], p2_r.at[s, (slot + d) % 4])

        half = kv.at[zz, :, c]
        send(half, half, c_s.at[s], c_r.at[s], dev(x, y, z, 1 - c))

    scale = HD ** (-0.5) * LOG2E

    def fold(parts, op):
        while len(parts) > 1:
            parts = [
                op(parts[i], parts[i + 1]) if i + 1 < len(parts) else parts[i]
                for i in range(0, len(parts), 2)
            ]
        return parts[0]

    def attend(s):
        zz = source(s)
        copy_wait(kv.at[zz, :, 0], c_r.at[s])

        def score(i):
            rows = pl.ds(i * QC, QC)
            tiles = []
            for k in range(0, CK, 256):
                keys = jnp.concatenate(
                    [kv[zz, 0].reshape(CK, HD)[k : k + 256], oh[zz, k : k + 256]], axis=1
                )
                scores = lax.dot_general(
                    qa[rows, :], keys, (((1,), (1,)), ((), ())), preferred_element_type=jnp.float32
                )
                tiles += [scores[:, :128], scores[:, 128:]]
            return tiles, jnp.max(fold(tiles, jnp.maximum), axis=1, keepdims=True)

        def gather(i, tiles, largest):
            rows = pl.ds(i * QC, QC)
            old = mm[rows, :]
            new = jnp.maximum(old, largest)
            weights = [jnp.exp2((t - new) * scale) for t in tiles]
            shrink = jnp.exp2((old - new) * scale)
            mm[rows, :] = new
            ll[rows, :] = ll[rows, :] * shrink + fold(weights, jnp.add)
            values = jnp.concatenate([kv[zz, 1].reshape(CK, HD), kv[zz, 2].reshape(CK, HD)], axis=1)
            low_weights = jnp.concatenate([w.astype(jnp.bfloat16) for w in weights], axis=1)
            sums = jnp.dot(low_weights, values, preferred_element_type=jnp.float32)
            oo[rows, :] = oo[rows, :] * jnp.concatenate([shrink, shrink], axis=1) + sums

        held = None
        for i in range(ROWS // QC):
            now = score(i)
            if held is not None:
                gather(i - 1, *held)
            held = now
        gather(ROWS // QC - 1, *held)

    def step(t, carry):
        attend(t)
        for stage, lead in zip((stage_three, stage_two, stage_one), LEADS):

            @pl.when(t + lead < NZ)
            def _(stage=stage, lead=lead):
                stage(t + lead)

        return carry

    stage_one(0)
    stage_two(0)
    stage_three(0)
    spread_queries()
    stage_one(1)
    stage_one(2)
    lend_queries()
    stage_two(1)
    stage_two(2)
    stage_one(3)
    ready_queries()
    for s in range(4, LEADS[2]):
        stage_one(s)
    for s in range(3, LEADS[1]):
        stage_two(s)
    lax.fori_loop(0, NZ, step, 0)

    def finish(i):
        rows = pl.ds(pl.multiple_of(i * 128, 128), 128)
        total = jnp.sum(ll[rows, :], axis=1, keepdims=True)
        share = mix[rows, :]
        both = oo[rows, :] / total
        ro[i] = (share * both[:, HD:] + (1.0 - share) * both[:, :HD]).astype(jnp.bfloat16)

    e_lanes = pl.ds(4 * HD, HD)

    far, near = 4 - 4 * (z // 4), 4 * (z // 4)

    def finish_some(first, count):
        def one(i, carry):
            finish(first + i)
            return carry

        lax.fori_loop(0, count, one, 0)

    def return_lent(n):
        for j in range(4):
            send(
                ro.at[pl.ds(8, n), pl.ds(j * TB, TB), :], ox.at[pl.ds(3 * y, n), :, lanes(x)],
                rb_s.at[j], rb_r.at[y, x], dev(j, 3, z, c),
            )

    def return_own(first, h):
        finish_some(first, 4)
        slots, which = pl.ds(first, 4), first // 4

        @pl.when(last)
        def _():
            local(ro.at[slots, pl.ds(3 * TB, TB), :], ox.at[slots, :, e_lanes], re_r.at[which])
            for t in range(3):
                send(
                    ro.at[slots, pl.ds(t * TB, TB), :], ox.at[slots, :, e_lanes],
                    r1_s.at[h, t], re_r.at[which], dev(x, t, z, c),
                )

        @pl.when(jnp.logical_not(last))
        def _():
            mine = lanes(x)
            local(ro.at[slots, block(x), :], ox.at[slots, :, mine], r1_r.at[which, x])
            for d in range(1, 4):
                j = (x + d) % 4
                send(
                    ro.at[slots, block(j), :], ox.at[slots, :, mine],
                    r1_s.at[h, d - 1], r1_r.at[which, x], dev(j, y, z, c),
                )

    finish_some(8, 3)

    @pl.when(y < 2)
    def _():
        return_lent(3)

    @pl.when(y == 2)
    def _():
        return_lent(2)

    return_own(far, 0)
    return_own(near, 1)
    target = cols(out_ref, z, HZ)

    @pl.when(last)
    def _():
        for t in range(3):
            n = 3 if t < 2 else 2
            for i in range(4):
                copy_wait(ox.at[pl.ds(3 * t, n), :, lanes(i)], rb_r.at[t, i])

    def arrived(first):
        slots, which = pl.ds(first, 4), first // 4

        @pl.when(jnp.logical_not(last))
        def _():
            for i in range(4):
                copy_wait(ox.at[slots, :, lanes(i)], r1_r.at[which, i])

        copy_wait(ox.at[slots, :, e_lanes], re_r.at[which])

    arrived(far)
    for i in range(4):
        zz = far + (z + i) % 4
        send(ox.at[zz], target, r2_s.at[i], r2_r.at[z], dev(x, y, zz, c))
    arrived(near)
    for i in range(1, 4):
        zz = near + (z + i) % 4
        send(ox.at[zz], target, r2_s.at[3 + i], r2_r.at[z], dev(x, y, zz, c))
    local(ox.at[z], target, r2_r.at[z])

    for s in range(1, NZ):
        wait_send(zq.at[0], zq_s.at[s])
        wait_send(zx.at[0], zx_s.at[s])
        wait_send(zkv.at[0], zk_s.at[s])
    for d in range(1, 4):
        wait_send(hq.at[:, pl.ds(0, TB), :], pq_s.at[d])
        wait_send(zx, px_s.at[d])

    def left(s, carry):
        for d in range(1, 4):
            wait_send(hk.at[0, :, pl.ds(0, TB), :], p1_s.at[s, d])
        wait_send(kv.at[0, :, 0], c_s.at[s])

        wait_send(hk.at[0], p2_s.at[s, 0])

        @pl.when(last)
        def _():
            for d in range(1, 4):
                wait_send(kv.at[0, :, 0, pl.ds(2, 2), pl.ds(0, TB), :], e_s.at[s, d])
            wait_send(hk.at[0], p2_s.at[s, 2])

        @pl.when(jnp.logical_not(even))
        def _():
            wait_send(hk.at[0], p2_s.at[s, 1])

        @pl.when(y == 1)
        def _():
            wait_send(hk.at[0, :, pl.ds(0, TB), :], p1_s.at[s, 0])

        @pl.when(even)
        def _():
            wait_send(hk.at[0], p2_s.at[s, 1])
            wait_send(hk.at[0], e_s.at[s, 0])
            for d in range(1, 4):
                wait_send(hk.at[0, :, pl.ds(0, TB), :], p1e_s.at[s, d])

        return carry

    lax.fori_loop(0, NZ, left, 0)

    @pl.when(last)
    def _():
        for t in range(3):
            n = 3 if t < 2 else 2
            wait_send(hq.at[pl.ds(0, n)], bq_s.at[t])
            wait_send(hx.at[pl.ds(0, n)], bx_s.at[t])

    @pl.when(jnp.logical_not(last))
    def _():
        wait_send(hq.at[:, pl.ds(0, TB), :], pq_s.at[0])
        wait_send(zx, px_s.at[0])

        @pl.when(y < 2)
        def _():
            for j in range(4):
                wait_send(ro.at[pl.ds(0, 3), pl.ds(0, TB), :], rb_s.at[j])

        @pl.when(y == 2)
        def _():
            for j in range(4):
                wait_send(ro.at[pl.ds(0, 2), pl.ds(0, TB), :], rb_s.at[j])

    for h in range(2):
        for t in range(3):
            wait_send(ro.at[pl.ds(0, 4), pl.ds(0, TB), :], r1_s.at[h, t])
    for i in range(NZ - 1):
        wait_send(ox.at[0], r2_s.at[i])
    for i in range(NZ):
        copy_wait(ox.at[0], r2_r.at[i])


def on_device(query_src, key_src, value_src, value_edit, tile_mask, word_map, blend_table):
    bf, f32 = jnp.bfloat16, jnp.float32
    dma = pltpu.SemaphoreType.DMA
    anywhere = pl.BlockSpec(memory_space=pl.ANY)
    vmem = pl.BlockSpec(memory_space=pltpu.VMEM)
    return pl.pallas_call(
        body,
        out_shape=jax.ShapeDtypeStruct(query_src.shape, bf),
        in_specs=[anywhere] * 4 + [vmem] * 3,
        out_specs=vmem,
        scratch_shapes=[
            pltpu.VMEM((NZ, 8, 128), f32),
            pltpu.VMEM((NZ, TB, HZ * HD), bf),
            pltpu.VMEM((NZ, 8, 128), f32),
            pltpu.VMEM((NZ, 3, TB, HZ * HD), bf),
            pltpu.VMEM((NZ, 128, HD), bf),
            pltpu.VMEM((NZ, 4, 8, 128), f32),
            pltpu.VMEM((NZ, 3, 128, HD), bf),
            pltpu.VMEM((NZ, 3, 128, HD), bf),
            pltpu.VMEM((SLOTS, 128, HD), bf),
            pltpu.VMEM((SLOTS, 4, 8, 128), f32),
            pltpu.VMEM((NZ, 3, NC, 4, 128, HD), bf),
            pltpu.VMEM((NZ, CK, HD), bf),
            pltpu.VMEM((ROWS, 2 * HD), bf),
            pltpu.VMEM((ROWS, 128), f32),
            pltpu.VMEM((ROWS, 128), f32),
            pltpu.VMEM((ROWS, 128), f32),
            pltpu.VMEM((ROWS, 2 * HD), f32),
            pltpu.VMEM((SLOTS, 128, HD), bf),
            pltpu.VMEM((NZ, TB, HZ * HD), bf),
            dma((NZ,)), dma((NZ,)), dma((NZ,)), dma((NZ,)), dma((NZ,)), dma((NZ,)),
            dma((4,)), dma((4,)), dma((4,)), dma((4,)), dma((4,)), dma((4,)),
            dma((3,)), dma(()), dma((3,)), dma(()),
            dma((NZ, 4)), dma((NZ, 4)), dma((NZ, 4)),
            dma((NZ, 4)), dma((NZ, 3)), dma((NZ, 4)), dma((NZ, 4)), dma((NZ, 4)), dma((NZ,)), dma((NZ,)),
            dma((2, 3)), dma((2, 4)), dma((4,)), dma((3, 4)), dma((2,)),
            dma((NZ,)), dma((NZ,)),
        ],
        compiler_params=pltpu.CompilerParams(
            collective_id=0, has_side_effects=True, vmem_limit_bytes=VMEM_LIMIT
        ),
        cost_estimate=pl.CostEstimate(
            flops=4 * ROWS * 8192 * 256, bytes_accessed=8 * 1024 * 1024, transcendentals=ROWS * 8192
        ),
    )(query_src, key_src, value_src, value_edit, tile_mask, word_map.reshape(1, TB), blend_table.T)


def solution(mesh):
    return jax.shard_map(
        on_device,
        mesh=mesh,
        in_specs=(
            P(("seq", "head"), None),
            P(("seq", "head"), None),
            P(("seq", "head"), None),
            P(("seq", "head"), None),
            P("seq", None),
            P(("seq", "head")),
            P(),
        ),
        out_specs=P(("seq", "head"), None),
        check_vma=False,
    )
```

```python
import jax
import jax.numpy as jnp
from jax import lax
from jax.experimental import pallas as pl
from jax.experimental.pallas import tpu as pltpu
from jax.sharding import PartitionSpec as P

MESH = pl.DeviceIdType.MESH
HD = 128
NX, NY, NZ, NC = 4, 4, 8, 2
HZ = 5
TB = 32
SLOTS = 11
ROWS = SLOTS * 4 * TB
CK = 1024
QC = 704
MASKED = -(2.0**100)
OFFS = (0, 1, -1, 2, -2, 3, -3, 4)
VMEM_LIMIT = 60 * 1024 * 1024
LEADS = (2, 4, 6)
AHEAD = 7
LOG2E = 1.4426950408889634


def offset_of(s):
    half = (s + 1) // 2
    return half * (2 * (s % 2) - 1)


def copy_wait(ref, sem):
    pltpu.make_async_copy(ref, ref, sem).wait()


def body(
    q_ref, k_ref, v_ref, w_ref, mask_ref, word_ref, blend_ref, out_ref,
    ext_ref, zq, zx, zkv, hq, hx, hk, ek, qb, xb, kv, oh, qa, mix, mm, ll, oo, ro, ox,
    zq_s, zq_r, zx_s, zx_r, zk_s, zk_r,
    pq_s, pq_r, pqe_r, px_s, px_r, pxe_r, bq_s, bq_r, bx_s, bx_r,
    p1_s, p1_r, p1e_r, p1e_s, p2_s, p2_r, e_s, e_r, c_s, c_r,
    r1_s, r1_r, rb_s, rb_r, re_r, r2_s, r2_r,
):
    seq = lax.axis_index("seq")
    head = lax.axis_index("head")
    z = (seq // 8) * 2 + head // 4
    x = (seq // 2) % 4
    c = seq % 2
    y = head % 4
    last = y == 3
    even = y % 2 == 0
    slot = (y % 2) * 2 + y // 2

    def dev(dx, dy, dz, dc):
        return ((dz // 2) * 8 + dx * 2 + dc, (dz % 2) * 4 + dy)

    def send(src, dst, ss, rs, to):
        pltpu.make_async_remote_copy(
            src_ref=src, dst_ref=dst, send_sem=ss, recv_sem=rs, device_id=to, device_id_type=MESH
        ).start()

    def local(src, dst, rs):
        pltpu.make_async_copy(src, dst, rs).start()

    def wait_send(src, ss):
        copy_wait(src, ss)

    def cols(ref3, zz, count):
        return ref3.at[:, pl.ds(pl.multiple_of(zz * (HZ * HD), HD), count * HD)]

    def lanes(j):
        return pl.ds(pl.multiple_of(j * HD, HD), HD)

    def block(i):
        return pl.ds(pl.multiple_of(i * TB, TB), TB)

    barrier = pltpu.get_barrier_semaphore()
    for d in range(1, NZ):
        pl.semaphore_signal(barrier, inc=1, device_id=dev(x, y, (z + d) % NZ, c), device_id_type=MESH)
    for d in range(1, NX * NY):
        pl.semaphore_signal(
            barrier, inc=1, device_id=dev((x + d // 4) % 4, (y + d % 4) % 4, z, c), device_id_type=MESH
        )
    pl.semaphore_signal(barrier, inc=1, device_id=dev(x, y, z, 1 - c), device_id_type=MESH)

    words = blend_ref.shape[1]
    hit = lax.broadcasted_iota(jnp.int32, (words, TB), 0) == word_ref[...]
    shares = jnp.dot(
        blend_ref[...], hit.astype(jnp.float32),
        precision=lax.Precision.HIGHEST, preferred_element_type=jnp.float32,
    )
    mask_row = jnp.where(mask_ref[pl.ds(head // 2, 1), :] == 1, 0.0, MASKED).astype(jnp.float32)
    for i in range(NZ):
        ext_ref[i] = jnp.zeros((8, 128), jnp.float32)
        ext_ref[i, 0:1, :] = mask_row
        ext_ref[i, 1 : 1 + HZ, 0:TB] = shares[i * HZ : (i + 1) * HZ, :]
    row = lax.broadcasted_iota(jnp.int32, (CK, HD), 0)
    lane = lax.broadcasted_iota(jnp.int32, (CK, HD), 1)
    tile = (row // TB) % 4 * 8 + (row // 512) * 4 + (row // 128) % 2

    def fill_onehot(zz, carry):
        base = (zz // 2) * 32 + (zz % 2) * 2
        oh[zz] = jnp.where(lane - base == tile, 1.0, 0.0).astype(jnp.bfloat16)
        return carry

    lax.fori_loop(0, NZ, fill_onehot, 0)
    mm[...] = jnp.full(mm.shape, MASKED, jnp.float32)
    ll[...] = jnp.zeros(ll.shape, jnp.float32)

    def clear(i, carry):
        oo[pl.ds(pl.multiple_of(i * 128, 128), 128), :] = jnp.zeros((128, 2 * HD), jnp.float32)
        return carry

    lax.fori_loop(0, SLOTS, clear, 0)

    @pl.when(y >= 2)
    def _():
        qb[10] = jnp.zeros(qb.shape[1:], qb.dtype)
        xb[10] = jnp.zeros(xb.shape[1:], xb.dtype)

    @pl.when(last)
    def _():
        qb[8:10] = jnp.zeros((2,) + qb.shape[1:], qb.dtype)
        xb[8:10] = jnp.zeros((2,) + xb.shape[1:], xb.dtype)

    pl.semaphore_wait(barrier, NZ + NX * NY - 1)

    local(cols(q_ref, z, HZ), zq.at[z], zq_r.at[z])
    local(ext_ref.at[z], zx.at[z], zx_r.at[z])
    for s in range(1, NZ):
        to = (z - OFFS[s] + NZ) % NZ
        send(cols(q_ref, to, HZ), zq.at[z], zq_s.at[s], zq_r.at[z], dev(x, y, to, c))
        send(ext_ref.at[to], zx.at[z], zx_s.at[s], zx_r.at[z], dev(x, y, to, c))
    for i, ref in enumerate((k_ref, v_ref, w_ref)):
        local(cols(ref, z, HZ), zkv.at[z, i], zk_r.at[z])

    def stage_zero(s):
        to = (z - (OFFS[s] if isinstance(s, int) else offset_of(s)) + NZ) % NZ
        for i, ref in enumerate((k_ref, v_ref, w_ref)):
            send(cols(ref, to, HZ), zkv.at[z, i], zk_s.at[s], zk_r.at[z], dev(x, y, to, c))

    for s in range(1, 1 + AHEAD):
        stage_zero(s)

    def spread_queries():
        for i in range(NZ):
            copy_wait(zq.at[i], zq_r.at[i])
            copy_wait(zx.at[i], zx_r.at[i])

        def to_lines(qdst, xdst):
            local(zq.at[:, :, lanes(x)], qdst, pq_r.at[x])
            local(zx, xdst, px_r.at[x])
            for d in range(1, 4):
                j = (x + d) % 4
                send(zq.at[:, :, lanes(j)], qdst, pq_s.at[d], pq_r.at[x], dev(j, y, z, c))
                send(zx, xdst, px_s.at[d], px_r.at[x], dev(j, y, z, c))

        @pl.when(last)
        def _():
            to_lines(hq.at[:, block(x), :], hx.at[:, x])
            local(zq.at[:, :, pl.ds(4 * HD, HD)], qb.at[pl.ds(0, 8), pl.ds(3 * TB, TB), :], pqe_r.at[3])
            local(zx, xb.at[pl.ds(0, 8), 3], pxe_r.at[3])

        @pl.when(jnp.logical_not(last))
        def _():
            to_lines(qb.at[pl.ds(0, 8), block(x), :], xb.at[pl.ds(0, 8), x])
            send(
                zq.at[:, :, pl.ds(4 * HD, HD)], qb.at[pl.ds(0, 8), block(y), :],
                pq_s.at[0], pqe_r.at[y], dev(x, 3, z, c),
            )
            send(zx, xb.at[pl.ds(0, 8), y], px_s.at[0], pxe_r.at[y], dev(x, 3, z, c))

    def lend_queries():
        for i in range(4):
            copy_wait(hq.at[:, pl.ds(0, TB), :], pq_r.at[i])
            copy_wait(zx, px_r.at[i])

        @pl.when(last)
        def _():
            for t in range(3):
                n = 3 if t < 2 else 2
                send(hq.at[pl.ds(3 * t, n)], qb.at[pl.ds(8, n)], bq_s.at[t], bq_r, dev(x, t, z, c))
                send(hx.at[pl.ds(3 * t, n)], xb.at[pl.ds(8, n)], bx_s.at[t], bx_r, dev(x, t, z, c))
            for i in range(4):
                copy_wait(hq.at[:, pl.ds(0, TB), :], pqe_r.at[i])
                copy_wait(zx, pxe_r.at[i])

    def ready_queries():
        @pl.when(y < 2)
        def _():
            copy_wait(qb.at[pl.ds(8, 3)], bq_r)
            copy_wait(xb.at[pl.ds(8, 3)], bx_r)

        @pl.when(y == 2)
        def _():
            copy_wait(qb.at[pl.ds(8, 2)], bq_r)
            copy_wait(xb.at[pl.ds(8, 2)], bx_r)

        which = 1 + jnp.where(last, 4, x)
        sub = lax.broadcasted_iota(jnp.int32, (4, 8, 128), 1)
        diag = lax.broadcasted_iota(jnp.int32, (4, TB, 128), 1) == lax.broadcasted_iota(
            jnp.int32, (4, TB, 128), 2
        )

        def one(i, carry):
            rows = pl.ds(pl.multiple_of(i * 128, 128), 128)
            extra = xb[i]
            qa[rows, 0:HD] = qb[i]
            bias = jnp.broadcast_to(extra[:, 0:1, :], (4, TB, 128))
            qa[rows, HD : 2 * HD] = bias.reshape(128, 128).astype(jnp.bfloat16)
            shares = jnp.sum(jnp.where(sub == which, extra, 0.0), axis=1, keepdims=True)
            column = jnp.sum(jnp.where(diag, shares, 0.0), axis=2, keepdims=True)
            mix[rows, :] = jnp.broadcast_to(column, (4, TB, 128)).reshape(128, 128)
            return carry

        lax.fori_loop(0, SLOTS, one, 0)

    def source(s):
        return (z + (OFFS[s] if isinstance(s, int) else offset_of(s)) + NZ) % NZ

    def stage_one(s):
        zz = source(s)
        copy_wait(zkv.at[zz], zk_r.at[zz])

        def to_lines(dst):
            local(zkv.at[zz, :, :, lanes(x)], dst, p1_r.at[s, x])
            for d in range(1, 4):
                j = (x + d) % 4
                send(zkv.at[zz, :, :, lanes(j)], dst, p1_s.at[s, d], p1_r.at[s, x], dev(j, y, z, c))

        if AHEAD < 7:

            @pl.when(jnp.logical_and(s >= 1, s + AHEAD < NZ))
            def _():
                stage_zero(s + AHEAD)

        fifth = zkv.at[zz, :, :, pl.ds(4 * HD, HD)]

        @pl.when(last)
        def _():
            to_lines(hk.at[zz, :, block(x), :])
            local(fifth, kv.at[zz, :, c, 3, block(x), :], p1e_r.at[s, 3])

        @pl.when(jnp.logical_not(last))
        def _():
            to_lines(kv.at[zz, :, c, slot, block(x), :])

        @pl.when(y == 1)
        def _():
            send(fifth, kv.at[zz, :, c, 2, block(x), :], p1_s.at[s, 0], p1e_r.at[s, 2], dev(x, 3, z, c))

        @pl.when(even)
        def _():
            local(fifth, ek.at[zz, :, block(x), :], p1e_r.at[s, x])
            for d in range(1, 4):
                send(
                    fifth, ek.at[zz, :, block(x), :], p1e_s.at[s, d], p1e_r.at[s, x],
                    dev((x + d) % 4, y, z, c),
                )

    def stage_two(s):
        zz = source(s)
        piece = hk.at[zz, :, pl.ds(0, TB), :]
        for i in range(4):
            copy_wait(piece, p1_r.at[s, i])
        own = kv.at[zz, :, c, slot]

        @pl.when(last)
        def _():
            send(hk.at[zz], own, p2_s.at[s, 0], p2_r.at[s, 3], dev(x, 0, z, c))
            send(hk.at[zz], own, p2_s.at[s, 1], p2_r.at[s, 3], dev(x, 2, z, c))
            send(hk.at[zz], own, p2_s.at[s, 2], p2_r.at[s, 3], dev(x, 1, z, c))
            copy_wait(piece, p1e_r.at[s, 2])
            copy_wait(piece, p1e_r.at[s, 3])
            mine = kv.at[zz, :, c, pl.ds(2, 2), block(x), :]
            for d in range(1, 4):
                send(mine, mine, e_s.at[s, d], e_r.at[s, x], dev((x + d) % 4, 3, z, c))

        @pl.when(y == 1)
        def _():
            send(own, own, p2_s.at[s, 0], p2_r.at[s, slot], dev(x, 0, z, c))
            send(own, own, p2_s.at[s, 1], p2_r.at[s, slot], dev(x, 2, z, c))

        @pl.when(even)
        def _():
            send(own, own, p2_s.at[s, 0], p2_r.at[s, slot], dev(x, 1, z, c))
            send(own, own, p2_s.at[s, 1], p2_r.at[s, slot], dev(x, 2 - y, z, c))
            for i in range(4):
                copy_wait(piece, p1e_r.at[s, i])
            send(ek.at[zz], own, e_s.at[s, 0], p2_r.at[s, slot], dev(x, 3, z, c))

    def stage_three(s):
        zz = source(s)

        @pl.when(last)
        def _():
            for i in range(2):
                copy_wait(hk.at[zz], p2_r.at[s, i])
            for d in range(1, 4):
                copy_wait(kv.at[zz, :, 0, pl.ds(2, 2), pl.ds(0, TB), :], e_r.at[s, (x + d) % 4])

        @pl.when(jnp.logical_not(last))
        def _():
            for d in range(1, 4):
                copy_wait(hk.at[zz], p2_r.at[s, (slot + d) % 4])

        half = kv.at[zz, :, c]
        send(half, half, c_s.at[s], c_r.at[s], dev(x, y, z, 1 - c))

    scale = HD ** (-0.5) * LOG2E

    def fold(parts, op):
        while len(parts) > 1:
            parts = [
                op(parts[i], parts[i + 1]) if i + 1 < len(parts) else parts[i]
                for i in range(0, len(parts), 2)
            ]
        return parts[0]

    def attend(s):
        zz = source(s)
        copy_wait(kv.at[zz, :, 0], c_r.at[s])

        def score(i):
            rows = pl.ds(i * QC, QC)
            tiles = []
            for k in range(0, CK, 256):
                keys = jnp.concatenate(
                    [kv[zz, 0].reshape(CK, HD)[k : k + 256], oh[zz, k : k + 256]], axis=1
                )
                scores = lax.dot_general(
                    qa[rows, :], keys, (((1,), (1,)), ((), ())), preferred_element_type=jnp.float32
                )
                tiles += [scores[:, :128], scores[:, 128:]]
            return tiles, jnp.max(fold(tiles, jnp.maximum), axis=1, keepdims=True)

        def gather(i, tiles, largest):
            rows = pl.ds(i * QC, QC)
            old = mm[rows, :]
            new = jnp.maximum(old, largest)
            weights = [jnp.exp2((t - new) * scale) for t in tiles]
            shrink = jnp.exp2((old - new) * scale)
            mm[rows, :] = new
            ll[rows, :] = ll[rows, :] * shrink + fold(weights, jnp.add)
            values = jnp.concatenate([kv[zz, 1].reshape(CK, HD), kv[zz, 2].reshape(CK, HD)], axis=1)
            low_weights = jnp.concatenate([w.astype(jnp.bfloat16) for w in weights], axis=1)
            sums = jnp.dot(low_weights, values, preferred_element_type=jnp.float32)
            oo[rows, :] = oo[rows, :] * jnp.concatenate([shrink, shrink], axis=1) + sums

        held = None
        for i in range(ROWS // QC):
            now = score(i)
            if held is not None:
                gather(i - 1, *held)
            held = now
        gather(ROWS // QC - 1, *held)

    def step(t, carry):
        attend(t)
        for stage, lead in zip((stage_three, stage_two, stage_one), LEADS):

            @pl.when(t + lead < NZ)
            def _(stage=stage, lead=lead):
                stage(t + lead)

        return carry

    stage_one(0)
    stage_two(0)
    stage_three(0)
    spread_queries()
    stage_one(1)
    stage_one(2)
    lend_queries()
    stage_two(1)
    stage_two(2)
    stage_one(3)
    ready_queries()
    for s in range(4, LEADS[2]):
        stage_one(s)
    for s in range(3, LEADS[1]):
        stage_two(s)
    for s in range(1, LEADS[0]):
        stage_three(s)
    lax.fori_loop(0, NZ, step, 0)

    def finish(i):
        rows = pl.ds(pl.multiple_of(i * 128, 128), 128)
        total = jnp.sum(ll[rows, :], axis=1, keepdims=True)
        share = mix[rows, :]
        both = oo[rows, :] / total
        ro[i] = (share * both[:, HD:] + (1.0 - share) * both[:, :HD]).astype(jnp.bfloat16)

    e_lanes = pl.ds(4 * HD, HD)

    far, near = 4 - 4 * (z // 4), 4 * (z // 4)

    def finish_some(first, count):
        def one(i, carry):
            finish(first + i)
            return carry

        lax.fori_loop(0, count, one, 0)

    def return_lent(n):
        for j in range(4):
            send(
                ro.at[pl.ds(8, n), pl.ds(j * TB, TB), :], ox.at[pl.ds(3 * y, n), :, lanes(x)],
                rb_s.at[j], rb_r.at[y, x], dev(j, 3, z, c),
            )

    def return_own(first, h):
        finish_some(first, 4)
        slots, which = pl.ds(first, 4), first // 4

        @pl.when(last)
        def _():
            local(ro.at[slots, pl.ds(3 * TB, TB), :], ox.at[slots, :, e_lanes], re_r.at[which])
            for t in range(3):
                send(
                    ro.at[slots, pl.ds(t * TB, TB), :], ox.at[slots, :, e_lanes],
                    r1_s.at[h, t], re_r.at[which], dev(x, t, z, c),
                )

        @pl.when(jnp.logical_not(last))
        def _():
            mine = lanes(x)
            local(ro.at[slots, block(x), :], ox.at[slots, :, mine], r1_r.at[which, x])
            for d in range(1, 4):
                j = (x + d) % 4
                send(
                    ro.at[slots, block(j), :], ox.at[slots, :, mine],
                    r1_s.at[h, d - 1], r1_r.at[which, x], dev(j, y, z, c),
                )

    finish_some(8, 3)

    @pl.when(y < 2)
    def _():
        return_lent(3)

    @pl.when(y == 2)
    def _():
        return_lent(2)

    return_own(far, 0)
    return_own(near, 1)
    target = cols(out_ref, z, HZ)

    @pl.when(last)
    def _():
        for t in range(3):
            n = 3 if t < 2 else 2
            for i in range(4):
                copy_wait(ox.at[pl.ds(3 * t, n), :, lanes(i)], rb_r.at[t, i])

    def arrived(first):
        slots, which = pl.ds(first, 4), first // 4

        @pl.when(jnp.logical_not(last))
        def _():
            for i in range(4):
                copy_wait(ox.at[slots, :, lanes(i)], r1_r.at[which, i])

        copy_wait(ox.at[slots, :, e_lanes], re_r.at[which])

    arrived(far)
    for i in range(4):
        zz = far + (z + i) % 4
        send(ox.at[zz], target, r2_s.at[i], r2_r.at[z], dev(x, y, zz, c))
    arrived(near)
    for i in range(1, 4):
        zz = near + (z + i) % 4
        send(ox.at[zz], target, r2_s.at[3 + i], r2_r.at[z], dev(x, y, zz, c))
    local(ox.at[z], target, r2_r.at[z])

    for s in range(1, NZ):
        wait_send(zq.at[0], zq_s.at[s])
        wait_send(zx.at[0], zx_s.at[s])
        wait_send(zkv.at[0], zk_s.at[s])
    for d in range(1, 4):
        wait_send(hq.at[:, pl.ds(0, TB), :], pq_s.at[d])
        wait_send(zx, px_s.at[d])

    def left(s, carry):
        for d in range(1, 4):
            wait_send(hk.at[0, :, pl.ds(0, TB), :], p1_s.at[s, d])
        wait_send(kv.at[0, :, 0], c_s.at[s])

        wait_send(hk.at[0], p2_s.at[s, 0])

        @pl.when(last)
        def _():
            for d in range(1, 4):
                wait_send(kv.at[0, :, 0, pl.ds(2, 2), pl.ds(0, TB), :], e_s.at[s, d])
            wait_send(hk.at[0], p2_s.at[s, 2])

        @pl.when(jnp.logical_not(even))
        def _():
            wait_send(hk.at[0], p2_s.at[s, 1])

        @pl.when(y == 1)
        def _():
            wait_send(hk.at[0, :, pl.ds(0, TB), :], p1_s.at[s, 0])

        @pl.when(even)
        def _():
            wait_send(hk.at[0], p2_s.at[s, 1])
            wait_send(hk.at[0], e_s.at[s, 0])
            for d in range(1, 4):
                wait_send(hk.at[0, :, pl.ds(0, TB), :], p1e_s.at[s, d])

        return carry

    lax.fori_loop(0, NZ, left, 0)

    @pl.when(last)
    def _():
        for t in range(3):
            n = 3 if t < 2 else 2
            wait_send(hq.at[pl.ds(0, n)], bq_s.at[t])
            wait_send(hx.at[pl.ds(0, n)], bx_s.at[t])

    @pl.when(jnp.logical_not(last))
    def _():
        wait_send(hq.at[:, pl.ds(0, TB), :], pq_s.at[0])
        wait_send(zx, px_s.at[0])

        @pl.when(y < 2)
        def _():
            for j in range(4):
                wait_send(ro.at[pl.ds(0, 3), pl.ds(0, TB), :], rb_s.at[j])

        @pl.when(y == 2)
        def _():
            for j in range(4):
                wait_send(ro.at[pl.ds(0, 2), pl.ds(0, TB), :], rb_s.at[j])

    for h in range(2):
        for t in range(3):
            wait_send(ro.at[pl.ds(0, 4), pl.ds(0, TB), :], r1_s.at[h, t])
    for i in range(NZ - 1):
        wait_send(ox.at[0], r2_s.at[i])
    for i in range(NZ):
        copy_wait(ox.at[0], r2_r.at[i])


def on_device(query_src, key_src, value_src, value_edit, tile_mask, word_map, blend_table):
    bf, f32 = jnp.bfloat16, jnp.float32
    dma = pltpu.SemaphoreType.DMA
    anywhere = pl.BlockSpec(memory_space=pl.ANY)
    vmem = pl.BlockSpec(memory_space=pltpu.VMEM)
    return pl.pallas_call(
        body,
        out_shape=jax.ShapeDtypeStruct(query_src.shape, bf),
        in_specs=[anywhere] * 4 + [vmem] * 3,
        out_specs=vmem,
        scratch_shapes=[
            pltpu.VMEM((NZ, 8, 128), f32),
            pltpu.VMEM((NZ, TB, HZ * HD), bf),
            pltpu.VMEM((NZ, 8, 128), f32),
            pltpu.VMEM((NZ, 3, TB, HZ * HD), bf),
            pltpu.VMEM((NZ, 128, HD), bf),
            pltpu.VMEM((NZ, 4, 8, 128), f32),
            pltpu.VMEM((NZ, 3, 128, HD), bf),
            pltpu.VMEM((NZ, 3, 128, HD), bf),
            pltpu.VMEM((SLOTS, 128, HD), bf),
            pltpu.VMEM((SLOTS, 4, 8, 128), f32),
            pltpu.VMEM((NZ, 3, NC, 4, 128, HD), bf),
            pltpu.VMEM((NZ, CK, HD), bf),
            pltpu.VMEM((ROWS, 2 * HD), bf),
            pltpu.VMEM((ROWS, 128), f32),
            pltpu.VMEM((ROWS, 128), f32),
            pltpu.VMEM((ROWS, 128), f32),
            pltpu.VMEM((ROWS, 2 * HD), f32),
            pltpu.VMEM((SLOTS, 128, HD), bf),
            pltpu.VMEM((NZ, TB, HZ * HD), bf),
            dma((NZ,)), dma((NZ,)), dma((NZ,)), dma((NZ,)), dma((NZ,)), dma((NZ,)),
            dma((4,)), dma((4,)), dma((4,)), dma((4,)), dma((4,)), dma((4,)),
            dma((3,)), dma(()), dma((3,)), dma(()),
            dma((NZ, 4)), dma((NZ, 4)), dma((NZ, 4)),
            dma((NZ, 4)), dma((NZ, 3)), dma((NZ, 4)), dma((NZ, 4)), dma((NZ, 4)), dma((NZ,)), dma((NZ,)),
            dma((2, 3)), dma((2, 4)), dma((4,)), dma((3, 4)), dma((2,)),
            dma((NZ,)), dma((NZ,)),
        ],
        compiler_params=pltpu.CompilerParams(
            collective_id=0, has_side_effects=True, vmem_limit_bytes=VMEM_LIMIT
        ),
        cost_estimate=pl.CostEstimate(
            flops=4 * ROWS * 8192 * 256, bytes_accessed=8 * 1024 * 1024, transcendentals=ROWS * 8192
        ),
    )(query_src, key_src, value_src, value_edit, tile_mask, word_map.reshape(1, TB), blend_table.T)


def solution(mesh):
    return jax.shard_map(
        on_device,
        mesh=mesh,
        in_specs=(
            P(("seq", "head"), None),
            P(("seq", "head"), None),
            P(("seq", "head"), None),
            P(("seq", "head"), None),
            P("seq", None),
            P(("seq", "head")),
            P(),
        ),
        out_specs=P(("seq", "head"), None),
        check_vma=False,
    )
```
